32 devices in a mesh: seq: 8 (over z, x), head: 4 (over y, core).
Axes of the slice: x: 2, y: 2, z: 4, core: 2. Of those that a mesh axis runs over, the one named last changes fastest.
Arguments:
- out_grad: bfloat16 [1024, 768], P('seq', 'head'), may hold values from -6 to 6
- expert_of: int32 [1024], P('seq'), may hold values from 0 to 7, as said below
- counts: int32 [8, 8], P(None, 'seq'), may hold values from 0 to 40, as said below
- w_up: bfloat16 [8, 768, 3072], P('seq', None, 'head'), may hold values from -0.21875 to 0.21875
- w_down: bfloat16 [8, 3072, 768], P('seq', 'head'), may hold values from -0.109375 to 0.109375
- pre_act: bfloat16 [2560, 3072], P('seq', 'head'), may hold values from -6 to 6
- queries: bfloat16 [1024, 1024], P('seq', 'head'), may hold values from -6 to 6
- keys: bfloat16 [1024, 1024], P('seq', 'head'), may hold values from -6 to 6
- values: bfloat16 [1024, 1024], P('seq', 'head'), may hold values from -6 to 6
- w_out: bfloat16 [1024, 768], P('head'), may hold values from -0.1875 to 0.1875
Outputs:
- grad_hidden: bfloat16 [1024, 768], P('seq')
- grad_queries: bfloat16 [1024, 1024], P('seq', 'head')
- grad_keys: bfloat16 [1024, 1024], P('seq', 'head')
- grad_values: bfloat16 [1024, 1024], P('seq', 'head')
The draws below stay inside these ranges and needn't reach their ends.
Inputs may be any that keep to these rules, and one draw needn't show every extreme that they name: `expert_of`: in each aligned block of 128 tokens at most 40 tokens name one expert; one expert, the same for every block, is named by exactly 40 tokens of every block, and every other expert by fewer than 40 tokens of a block. counts[s, e] is the number of tokens of block s that name expert e.
All inputs are finite; a program needn't handle non-finite values.
Results may differ from the reference program's by a relative error of at most 0.014.
Values may be sent and summed in bfloat16 or wider, within the bound.
A program may use at most 64 MiB of HBM per device.

```python
import math
import jax
import jax.numpy as jnp
from jax import lax

D = 768
FF = 3072
HD = 256
TOK_DEV = 128
HEADS = 4
EXPERTS = 8
TOKENS = 1024
CAP = 40
SLOTS = 320
N_HEAD = 4


def route_table(key):
    base_key = jax.random.fold_in(key, 7)
    hot_key, block_key = jax.random.split(base_key)
    hot_expert = jax.random.randint(hot_key, (), 0, EXPERTS)
    block_keys = jax.random.split(block_key, EXPERTS)
    spare_slots = (EXPERTS - 1) * (CAP - 1)

    def one_block(one_key):
        slot_key, order_key = jax.random.split(one_key)
        slot_order = jax.random.permutation(slot_key, spare_slots)
        others = slot_order[:TOK_DEV - CAP] // (CAP - 1)
        others = (others + (others >= hot_expert).astype(jnp.int32)).astype(jnp.int32)
        assigned = jnp.concatenate([jnp.full((CAP,), hot_expert, jnp.int32), others])
        position = jax.random.permutation(order_key, TOK_DEV)
        return assigned[position]
    return jax.vmap(one_block)(block_keys).astype(jnp.int32)


def draw_expert_of(key, part):
    return route_table(key).reshape(-1)


def draw_counts(key, part):
    routes = route_table(key)
    matches = routes[:, :, None] == jnp.arange(EXPERTS, dtype=jnp.int32)[None, None, :]
    return jnp.sum(matches.astype(jnp.int32), axis=1)


def levels(own_key, extent, cuts, smallest, top_value):
    gain = 1.0
    for dim, shards_of in cuts:
        steps = jax.random.uniform(jax.random.fold_in(jax.random.fold_in(own_key, 6), dim), (shards_of,), jnp.float32, smallest / len(cuts), top_value / len(cuts))
        gain = gain * jnp.repeat(jnp.exp(steps), extent[dim] // shards_of).reshape((-1,) + (1,) * (len(extent) - 1 - dim))
    return gain


def gaussian(key, dims, scale, bound, cuts=(), held_as=jnp.bfloat16):
    array = scale * jax.random.normal(key, dims, jnp.float32)
    if cuts:
        array = array * levels(key, dims, cuts, -0.22, 0.18)
    return jnp.clip(array, -bound, bound).astype(held_as)


def setup_inputs(seed: int = 0) -> dict:
    seeds = jax.random.split(jax.random.key(seed), 11)
    return {
        "out_grad": gaussian(seeds[0], (TOKENS, D), 1.0, 6.0, ((0, 8), (1, 4))),
        "expert_of": draw_expert_of(jax.random.fold_in(seeds[10], 71), 0),
        "counts": draw_counts(jax.random.fold_in(seeds[10], 71), 0),
        "w_up": gaussian(seeds[3], (EXPERTS, D, FF), D ** -0.5, 0.21875, ((0, 8), (2, 4))),
        "w_down": gaussian(seeds[4], (EXPERTS, FF, D), FF ** -0.5, 0.109375, ((0, 8), (1, 4))),
        "pre_act": gaussian(seeds[5], (EXPERTS * SLOTS, FF), 1.0, 6.0, ((0, 8), (1, 4))),
        "queries": gaussian(seeds[6], (TOKENS, HEADS * HD), 1.0, 6.0, ((0, 8), (1, 4))),
        "keys": gaussian(seeds[7], (TOKENS, HEADS * HD), 1.0, 6.0, ((0, 8), (1, 4))),
        "values": gaussian(seeds[8], (TOKENS, HEADS * HD), 1.0, 6.0, ((0, 8), (1, 4))),
        "w_out": gaussian(seeds[9], (HEADS * HD, D), (HEADS * HD) ** -0.5, 0.1875, ((0, 4),)),
    }


def reference(out_grad, expert_of, counts, w_up, w_down, pre_act, queries, keys, values, w_out):
    blocks = expert_of.reshape(EXPERTS, TOK_DEV)
    onehot = (blocks[:, :, None] == jnp.arange(EXPERTS, dtype=jnp.int32)[None, None, :]).astype(jnp.int32)
    token_rank = lax.optimization_barrier(jnp.sum((jnp.cumsum(onehot, axis=1) - 1) * onehot, axis=2))
    offsets = jnp.cumsum(counts, axis=0) - counts
    base_row = jnp.take_along_axis(offsets, blocks, axis=1)
    packed = (blocks * SLOTS + base_row + token_rank).reshape(-1).astype(jnp.int32)
    row_table = jnp.full((EXPERTS * SLOTS,), TOKENS, jnp.int32).at[packed].set(jnp.arange(TOKENS, dtype=jnp.int32))
    padded = jnp.concatenate([out_grad, jnp.zeros((1, D), out_grad.dtype)], axis=0)
    rows_in = padded[row_table].reshape(EXPERTS, SLOTS, D)
    pre_blocks = pre_act.reshape(EXPERTS, SLOTS, FF)
    quarter = FF // N_HEAD

    def expert_step(inputs):
        row_block, pre_block, up_weight, down_weight = inputs
        middle = jnp.dot(row_block, down_weight.T, preferred_element_type=jnp.float32)
        mid_grad = jnp.where(pre_block > 0, middle, jnp.zeros_like(middle)).astype(jnp.bfloat16)
        summed = jnp.zeros((SLOTS, D), jnp.float32)
        for part_index in range(N_HEAD):
            lower = part_index * quarter
            term = jnp.dot(mid_grad[:, lower:lower + quarter], up_weight[:, lower:lower + quarter].T, preferred_element_type=jnp.float32).astype(jnp.bfloat16)
            term = lax.optimization_barrier(term)
            summed = summed + term.astype(jnp.float32)
        return summed.astype(jnp.bfloat16)
    expert_packed = lax.map(expert_step, (rows_in, pre_blocks, w_up, w_down))
    expert_grad = expert_packed.reshape(EXPERTS * SLOTS, D)[packed]
    grad_hidden = (out_grad.astype(jnp.float32) + expert_grad.astype(jnp.float32)).astype(jnp.bfloat16)
    head_grad = jnp.dot(grad_hidden, w_out.T, preferred_element_type=jnp.float32).astype(jnp.bfloat16)
    query_heads = queries.astype(jnp.float32).reshape(TOKENS, HEADS, HD)
    key_heads = keys.astype(jnp.float32).reshape(TOKENS, HEADS, HD)
    value_heads = values.astype(jnp.float32).reshape(TOKENS, HEADS, HD)
    grad_heads = head_grad.astype(jnp.float32).reshape(TOKENS, HEADS, HD)
    key_state = jnp.einsum('tha,thb->hab', key_heads, value_heads)
    query_state = jnp.einsum('tha,thb->hab', query_heads, grad_heads)
    key_round = lax.optimization_barrier(key_state.astype(jnp.bfloat16)).astype(jnp.float32)
    query_round = lax.optimization_barrier(query_state.astype(jnp.bfloat16)).astype(jnp.float32)
    scaling = 1.0 / math.sqrt(HD * TOKENS)
    grad_queries = (scaling * jnp.einsum('thb,hab->tha', grad_heads, key_round)).reshape(TOKENS, HEADS * HD)
    grad_keys = (scaling * jnp.einsum('thb,hab->tha', value_heads, query_round)).reshape(TOKENS, HEADS * HD)
    grad_values = (scaling * jnp.einsum('tha,hab->thb', key_heads, query_round)).reshape(TOKENS, HEADS * HD)
    return (grad_hidden, grad_queries.astype(jnp.bfloat16), grad_keys.astype(jnp.bfloat16), grad_values.astype(jnp.bfloat16))
```

```python
import functools
import math

import jax
import jax.numpy as jnp
from jax import lax
from jax.experimental import pallas as pl
from jax.experimental.pallas import tpu as pltpu
from jax.sharding import PartitionSpec as P

MESH = pl.DeviceIdType.MESH
F32 = jnp.float32
BF16 = jnp.bfloat16
ROWS = 16


def iota(shape, dim):
    return lax.broadcasted_iota(jnp.int32, shape, dim)


def nn(a, b):
    return jnp.dot(a, b, preferred_element_type=F32)


def nt(a, b):
    return lax.dot_general(a, b, (((1,), (1,)), ((), ())), preferred_element_type=F32)


def kernel(
    n, cap, pad, scaling,
    og_ref, expert_ref, counts_ref, up_hbm, down_hbm, pre_hbm, q_ref, k_ref, v_ref, wout_hbm,
    gh_out, gq_out, gk_out, gv_out,
    up, down, pre, wout, mask, wide, wide_in, xsend, x, hsum, hsend, hrecv, ysend, yrecv,
    rsend, ret, eg, eg_in, gh, ks_send, ks_recv, ks, qs_send, qs_recv, qs,
    load_sem, one_send, one_recv, disp_send, disp_recv, ax_send, ax_recv, as_send, as_recv,
    ret_send, ret_recv, st_send, st_recv,
):
    s = lax.axis_index("seq")
    h = lax.axis_index("head")
    c = lax.rem(h, 2)
    y = lax.div(h, 2)
    sib = (s, h + 1 - 2 * c)
    far = (s, lax.rem(h + 2, 4))
    m = n // 2
    tok, width = og_ref.shape
    pair = 2 * width
    rows = m * pad
    depth = x.shape[2]
    piece = ks.shape[1]
    mine = pl.ds(pl.multiple_of(y * pair, 128), pair)
    other = pl.ds(pl.multiple_of((1 - y) * pair, 128), pair)
    parity = lax.rem(s + c, 2)

    def send(src, dst, ssem, rsem, to):
        return pltpu.make_async_remote_copy(
            src_ref=src, dst_ref=dst, send_sem=ssem, recv_sem=rsem, device_id=to, device_id_type=MESH
        )

    barrier = pltpu.get_barrier_semaphore()
    peers = [lax.rem(s + d, n) for d in range(1, n)]
    for p in peers:
        pl.semaphore_signal(barrier, inc=1, device_id=(p, h), device_id_type=MESH)
    for to in (sib, far):
        pl.semaphore_signal(barrier, inc=1, device_id=to, device_id_type=MESH)
    loads = [
        pltpu.make_async_copy(src, dst, load_sem.at[i])
        for i, (src, dst) in enumerate(
            ((pre_hbm, pre), (down_hbm.at[0], down), (up_hbm.at[0], up), (wout_hbm, wout))
        )
    ]
    for load in loads:
        load.start()

    place = (iota((width, pair), 1) == iota((width, pair), 0) + c * width).astype(BF16)
    wide[...] = nn(og_ref[...], place).astype(BF16)

    pl.semaphore_wait(barrier, n + 1)
    pending = []

    def start(copy):
        copy.start()
        pending.append(copy)
        return copy

    gather_wide = start(send(wide, wide_in, one_send.at[0], one_recv.at[0], sib))

    e_row = expert_ref[...]
    eye = iota((tok, tok), 0) == iota((tok, tok), 1)
    e_col = jnp.sum(jnp.where(eye, e_row, 0), axis=1, keepdims=True)
    same = (e_col == e_row).astype(jnp.int32)
    below = iota((tok, tok), 0) < iota((tok, tok), 1)
    rank_row = jnp.sum(jnp.where(below, same, 0), axis=0, keepdims=True)
    above = iota((tok, tok), 1) < iota((tok, tok), 0)
    rank_col = jnp.sum(jnp.where(above, same, 0), axis=1, keepdims=True)
    live_row = lax.rem(e_row, 2) == parity
    slot_row = jnp.where(live_row, lax.div(e_row, 2) * pad + rank_row, -1)
    live_col = lax.rem(e_col, 2) == parity
    slot_col = jnp.where(live_col, lax.div(e_col, 2) * pad + rank_col, -1)
    scatter = (iota((rows, tok), 0) == slot_row).astype(BF16)
    combine = (iota((tok, rows), 1) == slot_col).astype(BF16)

    ks_part = nn(k_ref[...].T, v_ref[...]).astype(BF16)
    for p in range(n):
        ks_send[p] = ks_part[p * piece : (p + 1) * piece]

    gather_wide.wait_recv()
    full = wide[...] + wide_in[...]
    wide_in[...] = full
    blocks = nn(scatter, full).astype(BF16)
    for i in range(m):
        xsend[i] = blocks[i * pad : (i + 1) * pad]
    order = [lax.rem(s + c + 2 * j, n) for j in range(m)]
    for j, p in enumerate(order):
        if j == 0:
            @pl.when(c == 1)
            def _():
                send(
                    xsend.at[lax.div(p, 2)], x.at[c * m + lax.div(s, 2), :, mine],
                    disp_send.at[j], disp_recv.at[lax.div(s, 2)], (p, h),
                ).start()

            @pl.when(c == 0)
            def _():
                x[lax.div(s, 2), :, mine] = xsend[lax.div(s, 2)]
        else:
            start(send(
                xsend.at[lax.div(p, 2)], x.at[c * m + lax.div(s, 2), :, mine],
                disp_send.at[j], disp_recv.at[lax.div(s, 2)], (p, h),
            ))

    def state_scatter(k, source, dest):
        for d, p in enumerate(peers):
            start(send(source.at[p], dest.at[s], st_send.at[k, d], st_recv.at[k, s], (p, h)))
        dest[s] = source[s]

    def state_sum(k, dest, total):
        for p in peers:
            send(dest.at[p], dest.at[p], st_send.at[k, 0], st_recv.at[k, p], (p, h)).wait_recv()
        acc = dest[0].astype(F32)
        for p in range(1, n):
            acc = acc + dest[p].astype(F32)
        total[s] = acc.astype(BF16)
        for d, p in enumerate(peers):
            start(send(
                total.at[s], total.at[s], st_send.at[k + 1, d], st_recv.at[k + 1, s], (p, h)
            ))

    def state_wait(k, total):
        for p in peers:
            send(total.at[p], total.at[p], st_send.at[k, 0], st_recv.at[k, p], (p, h)).wait_recv()

    state_scatter(0, ks_send, ks_recv)

    cnt_row = jnp.sum(
        jnp.where(iota((n, n), 0) == iota((n, n), 1), counts_ref[...], 0), axis=0, keepdims=True
    )
    slot = iota((2 * rows, 1), 0)
    block = lax.div(slot, pad)
    source = 2 * lax.rem(block, m) + lax.rem(lax.div(block, m) + s, 2)
    before = iota((2 * rows, n), 1) < source
    packed = jnp.sum(jnp.where(before, cnt_row, 0), axis=1, keepdims=True) + lax.rem(slot, pad)
    unpack = (iota((2 * rows, pre.shape[0]), 1) == packed).astype(BF16)
    loads[0].wait()
    mask[...] = nn(unpack, pre[...]).astype(BF16)

    for j, p in enumerate(order):
        i = lax.div(p, 2)
        spot = x.at[c * m + i, :, mine]

        def arrived():
            send(spot, spot, disp_send.at[j], disp_recv.at[i], (p, h)).wait_recv()

        if j == 0:
            pl.when(c == 1)(arrived)
        else:
            arrived()
        start(send(spot, spot, ax_send.at[j], ax_recv.at[j], far))
        start(send(spot, spot, as_send.at[j], as_recv.at[j], sib))
    for j, p in enumerate(order):
        spot = x.at[c * m + lax.div(p, 2), :, other]
        send(spot, spot, ax_send.at[j], ax_recv.at[j], far).wait_recv()
        start(send(spot, spot, as_send.at[m + j], as_recv.at[m + j], sib))

    loads[1].wait()
    loads[2].wait()

    def expert(cls):
        at = pl.ds(cls * m, m)
        xs = x[at].reshape(rows, depth)
        middle = nt(xs, down[...])
        live = mask[pl.ds(pl.multiple_of(cls * rows, ROWS), rows), :]
        mid = jnp.where(live > 0, middle, 0.0).astype(BF16)
        return nt(mid, up[...])

    hsum[...] = expert(c)
    sib_order = [lax.rem(s + 1 - c + 2 * j, n) for j in range(m)]
    for j, p in enumerate(sib_order):
        for k, half in ((0, mine), (m, other)):
            spot = x.at[(1 - c) * m + lax.div(p, 2), :, half]
            send(spot, spot, as_send.at[k + j], as_recv.at[k + j], sib).wait_recv()
    hsend[...] = expert(1 - c).astype(BF16)
    pair_sum = start(send(hsend, hrecv, one_send.at[1], one_recv.at[1], sib))
    state_sum(0, ks_recv, ks)
    pair_sum.wait_recv()
    ysend[...] = (hsum[:, other] + hrecv[:, other].astype(F32)).astype(BF16)
    far_sum = start(send(ysend, yrecv, one_send.at[2], one_recv.at[2], far))
    own = hsum[:, mine] + hrecv[:, mine].astype(F32)
    far_sum.wait_recv()
    rsend[...] = (own + yrecv[...].astype(F32)).astype(BF16).reshape(m, pad, pair)

    for j, p in enumerate(order):
        i = lax.div(p, 2)
        if j == 0:
            @pl.when(c == 1)
            def _():
                send(
                    rsend.at[i], ret.at[lax.div(s, 2)], ret_send.at[j],
                    ret_recv.at[lax.div(s, 2)], (p, h),
                ).start()

            @pl.when(c == 0)
            def _():
                ret[lax.div(s, 2)] = rsend[lax.div(s, 2)]
        else:
            start(send(
                rsend.at[i], ret.at[lax.div(s, 2)], ret_send.at[j],
                ret_recv.at[lax.div(s, 2)], (p, h),
            ))
    loads[3].wait()
    q_t = q_ref[...].T
    for j, p in enumerate(order):
        i = lax.div(p, 2)

        def arrived():
            send(ret.at[i], ret.at[i], ret_send.at[j], ret_recv.at[i], (p, h)).wait_recv()

        if j == 0:
            pl.when(c == 1)(arrived)
        else:
            arrived()
    share = nn(combine, ret[...].reshape(rows, pair))
    eg[...] = share.astype(BF16)
    pair_grad = start(send(eg, eg_in, one_send.at[3], one_recv.at[3], sib))
    own = wide_in[...].astype(F32) + share
    pair_grad.wait_recv()
    gh[:, mine] = (own + eg_in[...].astype(F32)).astype(BF16)
    spot = gh.at[:, mine]
    far_grad = start(send(spot, spot, one_send.at[4], one_recv.at[4], far))
    state_wait(1, ks)
    spot = gh.at[:, other]
    send(spot, spot, one_send.at[4], one_recv.at[4], far).wait_recv()
    hidden = gh[...]
    head_grad = nt(hidden, wout[...]).astype(BF16)
    qs_part = nn(q_t, head_grad).astype(BF16)
    for p in range(n):
        qs_send[p] = qs_part[p * piece : (p + 1) * piece]
    state_scatter(2, qs_send, qs_recv)
    gh_out[...] = hidden
    dim = n * piece
    gq_out[...] = (scaling * nt(head_grad, ks[...].reshape(dim, dim))).astype(BF16)
    state_sum(2, qs_recv, qs)
    state_wait(3, qs)
    q_round = qs[...].reshape(dim, dim)
    gk_out[...] = (scaling * nt(v_ref[...], q_round)).astype(BF16)
    gv_out[...] = (scaling * nn(k_ref[...], q_round)).astype(BF16)

    for copy in pending:
        copy.wait_send()

    @pl.when(c == 1)
    def _():
        send(xsend.at[0], xsend.at[0], disp_send.at[0], disp_recv.at[0], sib).wait_send()
        send(rsend.at[0], rsend.at[0], ret_send.at[0], ret_recv.at[0], sib).wait_send()


def fused(out_grad, expert_of, counts, w_up, w_down, pre_act, queries, keys, values, w_out):
    n = lax.axis_size("seq")
    m = n // 2
    tok, width = out_grad.shape
    slots = pre_act.shape[0]
    cap = slots // n
    pad = -(-cap // ROWS) * ROWS
    rows = m * pad
    depth, hidden = w_up.shape[1:]
    dim = queries.shape[1]
    pair = 2 * width
    piece = dim // n
    scaling = 1.0 / math.sqrt(dim * tok * n)
    vmem = pl.BlockSpec(memory_space=pltpu.VMEM)
    hbm = pl.BlockSpec(memory_space=pl.ANY)
    dma = pltpu.SemaphoreType.DMA

    def buf(*shape, dtype=BF16):
        return pltpu.VMEM(shape, dtype)

    state = buf(n, piece, dim)
    out = jax.ShapeDtypeStruct((tok, dim), BF16)
    return pl.pallas_call(
        functools.partial(kernel, n, cap, pad, scaling),
        out_shape=(jax.ShapeDtypeStruct((tok, depth), BF16), out, out, out),
        in_specs=[vmem, vmem, vmem, hbm, hbm, hbm, vmem, vmem, vmem, hbm],
        out_specs=(vmem,) * 4,
        scratch_shapes=[
            buf(depth, hidden), buf(hidden, depth), buf(slots, hidden), buf(dim, depth),
            buf(2 * rows, hidden), buf(tok, pair), buf(tok, pair), buf(m, pad, pair),
            buf(n, pad, depth), buf(rows, depth, dtype=F32), buf(rows, depth), buf(rows, depth),
            buf(rows, pair), buf(rows, pair), buf(m, pad, pair), buf(m, pad, pair),
            buf(tok, pair), buf(tok, pair), buf(tok, depth),
            state, state, state, state, state, state,
            dma((4,)), dma((5,)), dma((5,)), dma((m,)), dma((m,)), dma((m,)), dma((m,)),
            dma((n,)), dma((n,)), dma((m,)), dma((m,)), dma((4, n)), dma((4, n)),
        ],
        compiler_params=pltpu.CompilerParams(
            collective_id=0, has_side_effects=True, vmem_limit_bytes=48 * 1024 * 1024
        ),
    )(
        out_grad, expert_of.reshape(1, tok), counts, w_up, w_down, pre_act,
        queries, keys, values, w_out,
    )


def step(*arrays):
    n, heads = lax.axis_size("seq"), lax.axis_size("head")
    width, dim = arrays[0].shape[1], arrays[6].shape[1]
    fits = heads == 4 and n % 2 == 0 and dim % (n * ROWS) == 0 and 2 * width % 128 == 0
    return (fused if fits else shards)(*arrays)


def shards(out_grad, expert_of, counts, w_up, w_down, pre_act, queries, keys, values, w_out):
    experts = lax.axis_size("seq")
    tok_rows = out_grad.shape[0]
    slot_count = pre_act.shape[0]
    capacity = slot_count // experts
    head_dim = queries.shape[1]
    scaling = 1.0 / math.sqrt(head_dim * tok_rows * experts)
    full_rows = lax.all_gather(out_grad, "head", axis=1, tiled=True)
    expert_ids = jnp.arange(experts, dtype=jnp.int32)
    onehot = (expert_of[:, None] == expert_ids[None, :]).astype(jnp.int32)
    token_rank = jnp.sum((jnp.cumsum(onehot, axis=0) - 1) * onehot, axis=1)
    slot_of = expert_of * capacity + token_rank
    token_of_slot = (
        jnp.full((experts * capacity,), tok_rows, jnp.int32)
        .at[slot_of]
        .set(jnp.arange(tok_rows, dtype=jnp.int32))
    )
    arrived = counts[:, 0]
    offsets = jnp.cumsum(arrived) - arrived
    arrived_total = jnp.sum(arrived)
    packed_ids = jnp.arange(slot_count, dtype=jnp.int32)
    source = jnp.sum((offsets[None, :] <= packed_ids[:, None]).astype(jnp.int32), axis=1) - 1
    within = packed_ids - offsets[source]
    packed_live = packed_ids < arrived_total
    flat_pos = jnp.where(packed_live, source * capacity + within, experts * capacity)
    down_local = w_down[0]
    up_local = w_up[0]
    padded = jnp.concatenate(
        [full_rows, jnp.zeros((1, full_rows.shape[1]), full_rows.dtype)], axis=0
    )
    received = lax.all_to_all(
        padded[token_of_slot].reshape(experts, capacity, full_rows.shape[1]),
        "seq",
        split_axis=0,
        concat_axis=0,
        tiled=True,
    )
    flat_rows = received.reshape(experts * capacity, received.shape[2])
    padded = jnp.concatenate(
        [flat_rows, jnp.zeros((1, flat_rows.shape[1]), flat_rows.dtype)], axis=0
    )
    middle = jnp.dot(padded[flat_pos], down_local.T, preferred_element_type=jnp.float32)
    mid_grad = jnp.where(pre_act > 0, middle, jnp.zeros_like(middle)).astype(jnp.bfloat16)
    hidden_part = jnp.dot(mid_grad, up_local.T, preferred_element_type=jnp.float32)
    slot_ids = jnp.arange(experts * capacity, dtype=jnp.int32)
    slot_source = slot_ids // capacity
    slot_rank = slot_ids % capacity
    slot_live = slot_rank < arrived[slot_source]
    slot_pos = jnp.where(slot_live, offsets[slot_source] + slot_rank, slot_count)
    share_packed = lax.psum_scatter(
        hidden_part.astype(jnp.bfloat16), "head", scatter_dimension=1, tiled=True
    )
    share_width = share_packed.shape[1]
    padded_grad = jnp.concatenate(
        [share_packed, jnp.zeros((1, share_packed.shape[1]), jnp.bfloat16)], axis=0
    )
    returned = lax.all_to_all(
        padded_grad[slot_pos].reshape(experts, capacity, share_packed.shape[1]),
        "seq",
        split_axis=0,
        concat_axis=0,
        tiled=True,
    )
    share_grad = returned.reshape(experts * capacity, share_width)[slot_of]
    expert_grad = lax.all_gather(share_grad, "head", axis=1, tiled=True)
    grad_hidden = (full_rows.astype(jnp.float32) + expert_grad.astype(jnp.float32)).astype(
        jnp.bfloat16
    )
    head_grad = jnp.dot(grad_hidden, w_out.T, preferred_element_type=jnp.float32).astype(
        jnp.bfloat16
    )
    query_part = jnp.dot(queries.T, head_grad, preferred_element_type=jnp.float32)
    key_state, query_state = lax.psum(
        (jnp.dot(keys.T, values, preferred_element_type=jnp.float32), query_part), "seq"
    )
    key_round = key_state.astype(jnp.bfloat16)
    query_round = query_state.astype(jnp.bfloat16)
    grad_queries = (
        scaling * jnp.dot(head_grad, key_round.T, preferred_element_type=jnp.float32)
    ).astype(jnp.bfloat16)
    grad_keys = (
        scaling * jnp.dot(values, query_round.T, preferred_element_type=jnp.float32)
    ).astype(jnp.bfloat16)
    grad_values = (scaling * jnp.dot(keys, query_round, preferred_element_type=jnp.float32)).astype(
        jnp.bfloat16
    )
    return (grad_hidden, grad_queries, grad_keys, grad_values)


def solution(mesh):
    return jax.shard_map(
        step,
        mesh=mesh,
        in_specs=(
            P("seq", "head"),
            P("seq"),
            P(None, "seq"),
            P("seq", None, "head"),
            P("seq", "head", None),
            P("seq", "head"),
            P("seq", "head"),
            P("seq", "head"),
            P("seq", "head"),
            P("head", None),
        ),
        out_specs=(P("seq", None), P("seq", "head"), P("seq", "head"), P("seq", "head")),
        check_vma=False,
    )
```

```python
import functools
import math

import jax
import jax.numpy as jnp
from jax import lax
from jax.experimental import pallas as pl
from jax.experimental.pallas import tpu as pltpu
from jax.sharding import PartitionSpec as P

MESH = pl.DeviceIdType.MESH
F32 = jnp.float32
BF16 = jnp.bfloat16
ROWS = 16


def iota(shape, dim):
    return lax.broadcasted_iota(jnp.int32, shape, dim)


def nn(a, b):
    return jnp.dot(a, b, preferred_element_type=F32)


def nt(a, b):
    return lax.dot_general(a, b, (((1,), (1,)), ((), ())), preferred_element_type=F32)


def kernel(
    n, pad, scaling,
    og_hbm, expert_hbm, counts_hbm, up_hbm, down_hbm, pre_hbm, q_hbm, k_hbm, v_hbm, wout_hbm,
    gh, gq_out, gk_out, gv_out,
    expert_of, counts, up, down, pre, wout, q, k, v, mask, grad_t, xsend, x, hsum, hsend, hrecv,
    ysend, yrecv, rsend, ret, eg, eg_in, gh_all, ks_send, ks_recv, ks, qs_send, qs_recv, qs,
    load_sem, one_send, one_recv, disp_send, disp_recv, ax_send, ax_recv, as_send, as_recv,
    hs_send, hs_recv, hy_send, hy_recv, ret_send, ret_recv, st_send, st_recv,
):
    s = lax.axis_index("seq")
    h = lax.axis_index("head")
    c = lax.rem(h, 2)
    y = lax.div(h, 2)
    sib = (s, h + 1 - 2 * c)
    far = (s, lax.rem(h + 2, 4))
    m = n // 2
    width, tok = og_hbm.shape
    pair = 2 * width
    rows = m * pad
    depth = x.shape[2]
    piece = ks.shape[1]
    mine = pl.ds(pl.multiple_of(y * pair, 128), pair)
    other = pl.ds(pl.multiple_of((1 - y) * pair, 128), pair)
    parity = lax.rem(s + c, 2)
    own_rows = pl.ds(pl.multiple_of(c * width, ROWS), width)
    sib_rows = pl.ds(pl.multiple_of((1 - c) * width, ROWS), width)

    def send(src, dst, ssem, rsem, to):
        return pltpu.make_async_remote_copy(
            src_ref=src, dst_ref=dst, send_sem=ssem, recv_sem=rsem, device_id=to, device_id_type=MESH
        )

    barrier = pltpu.get_barrier_semaphore()
    peers = [lax.rem(s + d, n) for d in range(1, n)]
    for p in peers:
        pl.semaphore_signal(barrier, inc=1, device_id=(p, h), device_id_type=MESH)
    for to in (sib, far):
        pl.semaphore_signal(barrier, inc=1, device_id=to, device_id_type=MESH)
    loads = {}
    for i, (name, src, dst) in enumerate((
        ("expert", expert_hbm, expert_of), ("grad", og_hbm, grad_t.at[own_rows]),
        ("k", k_hbm, k), ("v", v_hbm, v), ("counts", counts_hbm, counts), ("pre", pre_hbm, pre),
        ("down", down_hbm.at[0], down), ("up", up_hbm.at[0], up), ("wout", wout_hbm, wout),
        ("q", q_hbm, q),
    )):
        loads[name] = pltpu.make_async_copy(src, dst, load_sem.at[i])
        loads[name].start()

    pl.semaphore_wait(barrier, n + 1)
    pending = []

    def start(copy):
        copy.start()
        pending.append(copy)
        return copy

    start(send(og_hbm, grad_t.at[own_rows], one_send.at[0], one_recv.at[0], sib))

    loads["expert"].wait()
    e_row = expert_of[...]
    eye = iota((tok, tok), 0) == iota((tok, tok), 1)
    e_col = jnp.sum(jnp.where(eye, e_row, 0), axis=1, keepdims=True)
    same = (e_col == e_row).astype(jnp.int32)
    below = iota((tok, tok), 0) < iota((tok, tok), 1)
    rank_row = jnp.sum(jnp.where(below, same, 0), axis=0, keepdims=True)
    live_row = lax.rem(e_row, 2) == parity
    slot_row = jnp.where(live_row, lax.div(e_row, 2) * pad + rank_row, -1)
    scatter = (iota((rows, tok), 0) == slot_row).astype(BF16)

    loads["grad"].wait()
    spot = grad_t.at[sib_rows]
    send(spot, spot, one_send.at[0], one_recv.at[0], sib).wait_recv()
    blocks = nt(scatter, grad_t[...]).astype(BF16)
    for i in range(m):
        xsend[i] = blocks[i * pad : (i + 1) * pad]
    turns = [*range(1, m), 0]
    order = [(j, lax.rem(s + c + 2 * j, n)) for j in turns]
    for j, p in order:
        copy = send(
            xsend.at[lax.div(p, 2)], x.at[c * m + lax.div(s, 2), :, mine],
            disp_send.at[j], disp_recv.at[lax.div(s, 2)], (p, h),
        )
        if j == 0:
            pl.when(c == 1)(copy.start)

            @pl.when(c == 0)
            def _():
                x[lax.div(s, 2), :, mine] = xsend[lax.div(s, 2)]
        else:
            start(copy)

    loads["counts"].wait()
    slot = iota((2 * rows, 1), 0)
    block = lax.div(slot, pad)
    source = 2 * lax.rem(block, m) + lax.rem(lax.div(block, m) + s, 2)
    before = iota((2 * rows, n), 1) < source
    packed = jnp.sum(jnp.where(before, counts[...], 0), axis=1, keepdims=True) + lax.rem(slot, pad)
    unpack = (iota((2 * rows, pre.shape[0]), 1) == packed).astype(BF16)
    loads["pre"].wait()
    mask[...] = nn(unpack, pre[...]).astype(BF16)

    for j, p in order:
        i = lax.div(p, 2)
        spot = x.at[c * m + i, :, mine]
        copy = send(spot, spot, disp_send.at[j], disp_recv.at[i], (p, h))
        if j == 0:
            pl.when(c == 1)(copy.wait_recv)
        else:
            copy.wait_recv()
        start(send(spot, spot, ax_send.at[j], ax_recv.at[j], far))
        start(send(spot, spot, as_send.at[j], as_recv.at[j], sib))

    loads["k"].wait()
    loads["v"].wait()
    ks_part = nn(k[...].T, v[...]).astype(BF16)
    for p in range(n):
        ks_send[p] = ks_part[p * piece : (p + 1) * piece]

    def state_scatter(at, source, dest):
        for d, p in enumerate(peers):
            start(send(source.at[p], dest.at[s], st_send.at[at, d], st_recv.at[at, s], (p, h)))
        dest[s] = source[s]

    def state_sum(at, dest, total):
        for p in peers:
            send(dest.at[p], dest.at[p], st_send.at[at, 0], st_recv.at[at, p], (p, h)).wait_recv()
        acc = dest[0].astype(F32)
        for p in range(1, n):
            acc = acc + dest[p].astype(F32)
        total[s] = acc.astype(BF16)
        for d, p in enumerate(peers):
            start(send(
                total.at[s], total.at[s], st_send.at[at + 1, d], st_recv.at[at + 1, s], (p, h)
            ))

    def state_wait(at, total):
        for p in peers:
            send(total.at[p], total.at[p], st_send.at[at, 0], st_recv.at[at, p], (p, h)).wait_recv()

    state_scatter(0, ks_send, ks_recv)

    for j, p in order:
        spot = x.at[c * m + lax.div(p, 2), :, other]
        send(spot, spot, ax_send.at[j], ax_recv.at[j], far).wait_recv()
        start(send(spot, spot, as_send.at[m + j], as_recv.at[m + j], sib))

    loads["down"].wait()
    loads["up"].wait()

    def expert(cls):
        xs = x[pl.ds(cls * m, m)].reshape(rows, depth)
        middle = nt(xs, down[...])
        live = mask[pl.ds(pl.multiple_of(cls * rows, ROWS), rows), :]
        mid = jnp.where(live > 0, middle, 0.0).astype(BF16)
        return nt(mid, up[...]).reshape(m, pad, depth)

    hsum[...] = expert(c)
    sib_order = [(j, lax.rem(s + 1 - c + 2 * j, n)) for j in turns]
    for j, p in sib_order:
        for first, half in ((0, mine), (m, other)):
            spot = x.at[(1 - c) * m + lax.div(p, 2), :, half]
            send(spot, spot, as_send.at[first + j], as_recv.at[first + j], sib).wait_recv()
    hsend[...] = expert(1 - c).astype(BF16)
    for j, p in sib_order:
        i = lax.div(p, 2)
        start(send(hsend.at[i], hrecv.at[i], hs_send.at[j], hs_recv.at[j], sib))
    state_sum(0, ks_recv, ks)
    for j, p in order:
        i = lax.div(p, 2)
        spot = hrecv.at[i]
        send(spot, spot, hs_send.at[j], hs_recv.at[j], sib).wait_recv()
        ysend[i] = (hsum[i, :, other] + hrecv[i, :, other].astype(F32)).astype(BF16)
        start(send(ysend.at[i], yrecv.at[i], hy_send.at[j], hy_recv.at[j], far))

    for j, p in order:
        i = lax.div(p, 2)
        own = hsum[i, :, mine] + hrecv[i, :, mine].astype(F32)
        spot = yrecv.at[i]
        send(spot, spot, hy_send.at[j], hy_recv.at[j], far).wait_recv()
        rsend[i] = (own + yrecv[i].astype(F32)).astype(BF16)
        copy = send(
            rsend.at[i], ret.at[lax.div(s, 2)], ret_send.at[j], ret_recv.at[lax.div(s, 2)], (p, h)
        )
        if j == 0:
            pl.when(c == 1)(copy.start)

            @pl.when(c == 0)
            def _():
                ret[lax.div(s, 2)] = rsend[lax.div(s, 2)]
        else:
            start(copy)
    above = iota((tok, tok), 1) < iota((tok, tok), 0)
    rank_col = jnp.sum(jnp.where(above, same, 0), axis=1, keepdims=True)
    live_col = lax.rem(e_col, 2) == parity
    slot_col = jnp.where(live_col, lax.div(e_col, 2) * pad + rank_col, -1)
    combine = (iota((tok, rows), 1) == slot_col).astype(BF16)
    own = grad_t[...].astype(F32).T
    loads["wout"].wait()
    loads["q"].wait()
    q_t = q[...].T
    for j, p in order:
        i = lax.div(p, 2)
        copy = send(ret.at[i], ret.at[i], ret_send.at[j], ret_recv.at[i], (p, h))
        if j == 0:
            pl.when(c == 1)(copy.wait_recv)
        else:
            copy.wait_recv()
    share = nn(combine, ret[...].reshape(rows, pair))
    eg[...] = share.astype(BF16)
    start(send(eg, eg_in, one_send.at[1], one_recv.at[1], sib))
    own = own + share
    send(eg, eg_in, one_send.at[1], one_recv.at[1], sib).wait_recv()
    half = (own + eg_in[...].astype(F32)).astype(BF16)
    gh_all[:, mine] = half
    spot = gh_all.at[:, mine]
    start(send(spot, spot, one_send.at[2], one_recv.at[2], far))
    head_part = nt(half, wout[:, mine])
    state_wait(1, ks)
    spot = gh_all.at[:, other]
    send(spot, spot, one_send.at[2], one_recv.at[2], far).wait_recv()
    head_grad = (head_part + nt(gh_all[:, other], wout[:, other])).astype(BF16)
    qs_part = nn(q_t, head_grad).astype(BF16)
    for p in range(n):
        qs_send[p] = qs_part[p * piece : (p + 1) * piece]
    state_scatter(2, qs_send, qs_recv)
    gh[...] = gh_all[...]
    dim = n * piece
    gq_out[...] = (scaling * nt(head_grad, ks[...].reshape(dim, dim))).astype(BF16)
    state_sum(2, qs_recv, qs)
    state_wait(3, qs)
    q_round = qs[...].reshape(dim, dim)
    gk_out[...] = (scaling * nt(v[...], q_round)).astype(BF16)
    gv_out[...] = (scaling * nn(k[...], q_round)).astype(BF16)

    for copy in pending:
        copy.wait_send()

    @pl.when(c == 1)
    def _():
        send(xsend.at[0], xsend.at[0], disp_send.at[0], disp_recv.at[0], sib).wait_send()
        send(rsend.at[0], rsend.at[0], ret_send.at[0], ret_recv.at[0], sib).wait_send()


def write_out(*refs):
    count = len(refs) // 2
    sem = refs[-1]
    copies = [pltpu.make_async_copy(refs[i], refs[count + i], sem.at[i]) for i in range(count)]
    for copy in copies:
        copy.start()
    for copy in copies:
        copy.wait()


def fused(out_grad, expert_of, counts, w_up, w_down, pre_act, queries, keys, values, w_out):
    n = lax.axis_size("seq")
    m = n // 2
    tok, width = out_grad.shape
    slots = pre_act.shape[0]
    cap = slots // n
    pad = -(-cap // ROWS) * ROWS
    rows = m * pad
    depth, hidden = w_up.shape[1:]
    dim = queries.shape[1]
    pair = 2 * width
    piece = dim // n
    scaling = 1.0 / math.sqrt(dim * tok * n)
    vmem = pl.BlockSpec(memory_space=pltpu.VMEM)
    hbm = pl.BlockSpec(memory_space=pltpu.HBM)
    dma = pltpu.SemaphoreType.DMA

    def buf(*shape, dtype=BF16):
        return pltpu.VMEM(shape, dtype)

    state = buf(n, piece, dim)
    out = jax.ShapeDtypeStruct((tok, dim), BF16)
    outs = (jax.ShapeDtypeStruct((tok, depth), BF16), out, out, out)
    results = pl.pallas_call(
        functools.partial(kernel, n, pad, scaling),
        out_shape=outs,
        in_specs=[hbm] * 10,
        out_specs=(vmem,) * 4,
        scratch_shapes=[
            buf(1, tok, dtype=jnp.int32), buf(1, n, dtype=jnp.int32),
            buf(depth, hidden), buf(hidden, depth), buf(slots, hidden), buf(dim, depth),
            buf(tok, dim), buf(tok, dim), buf(tok, dim), buf(2 * rows, hidden),
            buf(pair, tok), buf(m, pad, pair), buf(n, pad, depth),
            buf(m, pad, depth, dtype=F32), buf(m, pad, depth), buf(m, pad, depth),
            buf(m, pad, pair), buf(m, pad, pair), buf(m, pad, pair), buf(m, pad, pair),
            buf(tok, pair), buf(tok, pair), buf(tok, depth),
            state, state, state, state, state, state,
            dma((10,)), dma((3,)), dma((3,)), dma((m,)), dma((m,)), dma((m,)), dma((m,)),
            dma((n,)), dma((n,)), dma((m,)), dma((m,)), dma((m,)), dma((m,)), dma((m,)), dma((m,)),
            dma((4, n)), dma((4, n)),
        ],
        compiler_params=pltpu.CompilerParams(
            collective_id=0, has_side_effects=True, vmem_limit_bytes=48 * 1024 * 1024
        ),
    )(*(pltpu.with_memory_space_constraint(operand, pltpu.HBM) for operand in (
        out_grad.T, expert_of.reshape(1, tok), counts.T, w_up, w_down, pre_act,
        queries, keys, values, w_out,
    )))
    return pl.pallas_call(
        write_out,
        out_shape=outs,
        in_specs=[vmem] * 4,
        out_specs=(hbm,) * 4,
        scratch_shapes=[dma((4,))],
    )(*results)


def step(*arrays):
    n, heads = lax.axis_size("seq"), lax.axis_size("head")
    width, dim = arrays[0].shape[1], arrays[6].shape[1]
    fits = heads == 4 and n % 2 == 0 and dim % (n * ROWS) == 0 and 2 * width % 128 == 0
    return (fused if fits else shards)(*arrays)


def shards(out_grad, expert_of, counts, w_up, w_down, pre_act, queries, keys, values, w_out):
    experts = lax.axis_size("seq")
    tok_rows = out_grad.shape[0]
    slot_count = pre_act.shape[0]
    capacity = slot_count // experts
    head_dim = queries.shape[1]
    scaling = 1.0 / math.sqrt(head_dim * tok_rows * experts)
    full_rows = lax.all_gather(out_grad, "head", axis=1, tiled=True)
    expert_ids = jnp.arange(experts, dtype=jnp.int32)
    onehot = (expert_of[:, None] == expert_ids[None, :]).astype(jnp.int32)
    token_rank = jnp.sum((jnp.cumsum(onehot, axis=0) - 1) * onehot, axis=1)
    slot_of = expert_of * capacity + token_rank
    token_of_slot = (
        jnp.full((experts * capacity,), tok_rows, jnp.int32)
        .at[slot_of]
        .set(jnp.arange(tok_rows, dtype=jnp.int32))
    )
    arrived = counts[:, 0]
    offsets = jnp.cumsum(arrived) - arrived
    arrived_total = jnp.sum(arrived)
    packed_ids = jnp.arange(slot_count, dtype=jnp.int32)
    source = jnp.sum((offsets[None, :] <= packed_ids[:, None]).astype(jnp.int32), axis=1) - 1
    within = packed_ids - offsets[source]
    packed_live = packed_ids < arrived_total
    flat_pos = jnp.where(packed_live, source * capacity + within, experts * capacity)
    down_local = w_down[0]
    up_local = w_up[0]
    padded = jnp.concatenate(
        [full_rows, jnp.zeros((1, full_rows.shape[1]), full_rows.dtype)], axis=0
    )
    received = lax.all_to_all(
        padded[token_of_slot].reshape(experts, capacity, full_rows.shape[1]),
        "seq",
        split_axis=0,
        concat_axis=0,
        tiled=True,
    )
    flat_rows = received.reshape(experts * capacity, received.shape[2])
    padded = jnp.concatenate(
        [flat_rows, jnp.zeros((1, flat_rows.shape[1]), flat_rows.dtype)], axis=0
    )
    middle = jnp.dot(padded[flat_pos], down_local.T, preferred_element_type=jnp.float32)
    mid_grad = jnp.where(pre_act > 0, middle, jnp.zeros_like(middle)).astype(jnp.bfloat16)
    hidden_part = jnp.dot(mid_grad, up_local.T, preferred_element_type=jnp.float32)
    slot_ids = jnp.arange(experts * capacity, dtype=jnp.int32)
    slot_source = slot_ids // capacity
    slot_rank = slot_ids % capacity
    slot_live = slot_rank < arrived[slot_source]
    slot_pos = jnp.where(slot_live, offsets[slot_source] + slot_rank, slot_count)
    share_packed = lax.psum_scatter(
        hidden_part.astype(jnp.bfloat16), "head", scatter_dimension=1, tiled=True
    )
    share_width = share_packed.shape[1]
    padded_grad = jnp.concatenate(
        [share_packed, jnp.zeros((1, share_packed.shape[1]), jnp.bfloat16)], axis=0
    )
    returned = lax.all_to_all(
        padded_grad[slot_pos].reshape(experts, capacity, share_packed.shape[1]),
        "seq",
        split_axis=0,
        concat_axis=0,
        tiled=True,
    )
    share_grad = returned.reshape(experts * capacity, share_width)[slot_of]
    expert_grad = lax.all_gather(share_grad, "head", axis=1, tiled=True)
    grad_hidden = (full_rows.astype(jnp.float32) + expert_grad.astype(jnp.float32)).astype(
        jnp.bfloat16
    )
    head_grad = jnp.dot(grad_hidden, w_out.T, preferred_element_type=jnp.float32).astype(
        jnp.bfloat16
    )
    query_part = jnp.dot(queries.T, head_grad, preferred_element_type=jnp.float32)
    key_state, query_state = lax.psum(
        (jnp.dot(keys.T, values, preferred_element_type=jnp.float32), query_part), "seq"
    )
    key_round = key_state.astype(jnp.bfloat16)
    query_round = query_state.astype(jnp.bfloat16)
    grad_queries = (
        scaling * jnp.dot(head_grad, key_round.T, preferred_element_type=jnp.float32)
    ).astype(jnp.bfloat16)
    grad_keys = (
        scaling * jnp.dot(values, query_round.T, preferred_element_type=jnp.float32)
    ).astype(jnp.bfloat16)
    grad_values = (scaling * jnp.dot(keys, query_round, preferred_element_type=jnp.float32)).astype(
        jnp.bfloat16
    )
    return (grad_hidden, grad_queries, grad_keys, grad_values)


def solution(mesh):
    return jax.shard_map(
        step,
        mesh=mesh,
        in_specs=(
            P("seq", "head"),
            P("seq"),
            P(None, "seq"),
            P("seq", None, "head"),
            P("seq", "head", None),
            P("seq", "head"),
            P("seq", "head"),
            P("seq", "head"),
            P("seq", "head"),
            P("head", None),
        ),
        out_specs=(P("seq", None), P("seq", "head"), P("seq", "head"), P("seq", "head")),
        check_vma=False,
    )
```

```python
import functools
import math

import jax
import jax.numpy as jnp
from jax import lax
from jax.experimental import pallas as pl
from jax.experimental.pallas import tpu as pltpu
from jax.sharding import PartitionSpec as P

MESH = pl.DeviceIdType.MESH
F32 = jnp.float32
BF16 = jnp.bfloat16
ROWS = 16
VMEM_BYTES = 63 * 1024 * 1024


def iota(shape, dim):
    return lax.broadcasted_iota(jnp.int32, shape, dim)


def nn(a, b):
    return jnp.dot(a, b, preferred_element_type=F32)


def nt(a, b):
    return lax.dot_general(a, b, (((1,), (1,)), ((), ())), preferred_element_type=F32)


def kernel(
    n, pad, scaling,
    og_hbm, expert_hbm, counts_hbm, up_hbm, down_hbm, pre_hbm, q_hbm, k_hbm, v_hbm, wout_hbm,
    gh_out, gq_out, gk_out, gv_out,
    expert_of, counts, up, down, pre, wout, q, k, v, mask, grad_t, xsend, x, hsum,
    ysend, yrecv, rsend, ret, eg, eg_in, gh, ks_send, ks_recv, ks, qs_send, qs_recv, qs,
    gq, gk, gv,
    load_sem, one_send, one_recv, disp_send, disp_recv, ax_send, ax_recv,
    hy_send, hy_recv, ret_send, ret_recv, st_send, st_recv, out_sem,
):
    s = lax.axis_index("seq")
    h = lax.axis_index("head")
    c = lax.rem(h, 2)
    y = lax.div(h, 2)
    sib = (s, h + 1 - 2 * c)
    far = (s, lax.rem(h + 2, 4))
    m = n // 2
    width, tok = og_hbm.shape
    pair = 2 * width
    rows = m * pad
    depth = x.shape[2]
    piece = ks.shape[1]
    mine = pl.ds(pl.multiple_of(y * pair, 128), pair)
    other = pl.ds(pl.multiple_of((1 - y) * pair, 128), pair)
    parity = lax.rem(s + c, 2)
    own_rows = pl.ds(pl.multiple_of(c * width, ROWS), width)
    sib_rows = pl.ds(pl.multiple_of((1 - c) * width, ROWS), width)

    def send(src, dst, ssem, rsem, to):
        return pltpu.make_async_remote_copy(
            src_ref=src, dst_ref=dst, send_sem=ssem, recv_sem=rsem, device_id=to, device_id_type=MESH
        )

    barrier = pltpu.get_barrier_semaphore()
    peers = [lax.rem(s + d, n) for d in range(1, n)]
    for p in peers:
        pl.semaphore_signal(barrier, inc=1, device_id=(p, h), device_id_type=MESH)
    for to in (sib, far):
        pl.semaphore_signal(barrier, inc=1, device_id=to, device_id_type=MESH)
    loads = {}
    for i, (name, src, dst) in enumerate((
        ("expert", expert_hbm, expert_of), ("grad", og_hbm, grad_t.at[own_rows]),
        ("k", k_hbm, k), ("v", v_hbm, v), ("counts", counts_hbm, counts),
        ("pre", pre_hbm, pre.at[0]), ("down", down_hbm.at[0], down.at[0]),
        ("up", up_hbm.at[0], up.at[0]), ("wout", wout_hbm, wout),
        ("q", q_hbm, q),
    )):
        loads[name] = pltpu.make_async_copy(src, dst, load_sem.at[i])
        loads[name].start()

    pl.semaphore_wait(barrier, n + 1)
    pending = []

    def start(copy):
        copy.start()
        pending.append(copy)
        return copy

    start(send(og_hbm, grad_t.at[own_rows], one_send.at[0], one_recv.at[0], sib))
    swaps = [
        start(send(src, dst, one_send.at[3 + i], one_recv.at[3 + i], sib))
        for i, (src, dst) in enumerate((
            (pre_hbm, pre.at[1]), (down_hbm.at[0], down.at[1]), (up_hbm.at[0], up.at[1])
        ))
    ]

    loads["expert"].wait()
    e_row = expert_of[...]
    eye = iota((tok, tok), 0) == iota((tok, tok), 1)
    e_col = jnp.sum(jnp.where(eye, e_row, 0), axis=1, keepdims=True)
    same = (e_col == e_row).astype(jnp.int32)
    below = iota((tok, tok), 0) < iota((tok, tok), 1)
    rank_row = jnp.sum(jnp.where(below, same, 0), axis=0, keepdims=True)
    live_row = lax.rem(e_row, 2) == parity
    slot_row = jnp.where(live_row, lax.div(e_row, 2) * pad + rank_row, -1)
    scatter = (iota((rows, tok), 0) == slot_row).astype(BF16)

    loads["grad"].wait()
    spot = grad_t.at[sib_rows]
    send(spot, spot, one_send.at[0], one_recv.at[0], sib).wait_recv()
    blocks = nt(scatter, grad_t[...]).astype(BF16)
    for i in range(m):
        xsend[i] = blocks[i * pad : (i + 1) * pad]
    turns = [*range(1, m), 0]
    order = [(j, lax.rem(s + c + 2 * j, n)) for j in turns]
    for j, p in order:
        copy = send(
            xsend.at[lax.div(p, 2)], x.at[lax.div(s, 2), :, mine],
            disp_send.at[j], disp_recv.at[lax.div(s, 2)], (p, h),
        )
        if j == 0:
            pl.when(c == 1)(copy.start)

            @pl.when(c == 0)
            def _():
                x[lax.div(s, 2), :, mine] = xsend[lax.div(s, 2)]
        else:
            start(copy)

    loads["counts"].wait()
    slot = iota((rows, 1), 0)
    source = 2 * lax.div(slot, pad) + parity
    before = iota((rows, n), 1) < source
    packed = jnp.sum(jnp.where(before, counts[...], 0), axis=1, keepdims=True) + lax.rem(slot, pad)
    unpack = (iota((rows, pre.shape[1]), 1) == packed).astype(BF16)
    loads["pre"].wait()
    mask[0] = nn(unpack, pre[0]).astype(BF16)

    for j, p in order:
        i = lax.div(p, 2)
        spot = x.at[i, :, mine]
        copy = send(spot, spot, disp_send.at[j], disp_recv.at[i], (p, h))
        if j == 0:
            pl.when(c == 1)(copy.wait_recv)
        else:
            copy.wait_recv()
        start(send(spot, spot, ax_send.at[j], ax_recv.at[j], far))

    loads["k"].wait()
    loads["v"].wait()
    ks_part = nn(k[...].T, v[...]).astype(BF16)
    for p in range(n):
        ks_send[p] = ks_part[p * piece : (p + 1) * piece]

    def state_scatter(at, source, dest):
        for d, p in enumerate(peers):
            start(send(source.at[p], dest.at[s], st_send.at[at, d], st_recv.at[at, s], (p, h)))
        dest[s] = source[s]

    def state_sum(at, dest, total):
        for p in peers:
            send(dest.at[p], dest.at[p], st_send.at[at, 0], st_recv.at[at, p], (p, h)).wait_recv()
        acc = dest[0].astype(F32)
        for p in range(1, n):
            acc = acc + dest[p].astype(F32)
        total[s] = acc.astype(BF16)
        for d, p in enumerate(peers):
            start(send(
                total.at[s], total.at[s], st_send.at[at + 1, d], st_recv.at[at + 1, s], (p, h)
            ))

    def state_wait(at, total):
        for p in peers:
            send(total.at[p], total.at[p], st_send.at[at, 0], st_recv.at[at, p], (p, h)).wait_recv()

    state_scatter(0, ks_send, ks_recv)

    swaps[0].wait_recv()
    mask[1] = nn(unpack, pre[1]).astype(BF16)
    loads["down"].wait()
    swaps[1].wait_recv()
    ready = x[:, :, mine].reshape(rows, pair)
    middle = [nt(ready, down[u, :, mine]) for u in range(2)]
    loads["up"].wait()
    swaps[2].wait_recv()
    for j, p in order:
        spot = x.at[lax.div(p, 2), :, other]
        send(spot, spot, ax_send.at[j], ax_recv.at[j], far).wait_recv()
    ready = x[:, :, other].reshape(rows, pair)
    mid = [
        jnp.where(mask[u] > 0, middle[u] + nt(ready, down[u, :, other]), 0.0).astype(BF16)
        for u in range(2)
    ]
    ysend[...] = (nt(mid[0], up[0, other, :]) + nt(mid[1], up[1, other, :])).astype(BF16).reshape(
        m, pad, pair
    )
    for j, p in order:
        i = lax.div(p, 2)
        start(send(ysend.at[i], yrecv.at[i], hy_send.at[j], hy_recv.at[j], far))
    hsum[...] = (nt(mid[0], up[0, mine, :]) + nt(mid[1], up[1, mine, :])).reshape(m, pad, pair)
    state_sum(0, ks_recv, ks)

    for j, p in order:
        i = lax.div(p, 2)
        spot = yrecv.at[i]
        send(spot, spot, hy_send.at[j], hy_recv.at[j], far).wait_recv()
        rsend[i] = (hsum[i] + yrecv[i].astype(F32)).astype(BF16)
        copy = send(
            rsend.at[i], ret.at[lax.div(s, 2)], ret_send.at[j], ret_recv.at[lax.div(s, 2)], (p, h)
        )
        if j == 0:
            pl.when(c == 1)(copy.start)

            @pl.when(c == 0)
            def _():
                ret[lax.div(s, 2)] = rsend[lax.div(s, 2)]
        else:
            start(copy)
    above = iota((tok, tok), 1) < iota((tok, tok), 0)
    rank_col = jnp.sum(jnp.where(above, same, 0), axis=1, keepdims=True)
    live_col = lax.rem(e_col, 2) == parity
    slot_col = jnp.where(live_col, lax.div(e_col, 2) * pad + rank_col, -1)
    combine = (iota((tok, rows), 1) == slot_col).astype(BF16)
    own = grad_t[...].astype(F32).T
    loads["wout"].wait()
    loads["q"].wait()
    q_t = q[...].T
    for j, p in order:
        i = lax.div(p, 2)
        copy = send(ret.at[i], ret.at[i], ret_send.at[j], ret_recv.at[i], (p, h))
        if j == 0:
            pl.when(c == 1)(copy.wait_recv)
        else:
            copy.wait_recv()
    share = nn(combine, ret[...].reshape(rows, pair))
    eg[...] = share.astype(BF16)
    start(send(eg, eg_in, one_send.at[1], one_recv.at[1], sib))
    own = own + share
    send(eg, eg_in, one_send.at[1], one_recv.at[1], sib).wait_recv()
    half = (own + eg_in[...].astype(F32)).astype(BF16)
    gh[:, mine] = half
    spot = gh.at[:, mine]
    start(send(spot, spot, one_send.at[2], one_recv.at[2], far))
    head_part = nt(half, wout[:, mine])
    state_wait(1, ks)
    spot = gh.at[:, other]
    send(spot, spot, one_send.at[2], one_recv.at[2], far).wait_recv()
    head_grad = (head_part + nt(gh[:, other], wout[:, other])).astype(BF16)
    qs_part = nn(q_t, head_grad).astype(BF16)
    for p in range(n):
        qs_send[p] = qs_part[p * piece : (p + 1) * piece]
    state_scatter(2, qs_send, qs_recv)
    writes = []

    def write(src, dst):
        writes.append(pltpu.make_async_copy(src, dst, out_sem.at[len(writes)]))
        writes[-1].start()

    write(gh, gh_out)
    dim = n * piece
    gq[...] = (scaling * nt(head_grad, ks[...].reshape(dim, dim))).astype(BF16)
    write(gq, gq_out)
    state_sum(2, qs_recv, qs)
    state_wait(3, qs)
    q_round = qs[...].reshape(dim, dim)
    gk[...] = (scaling * nt(v[...], q_round)).astype(BF16)
    write(gk, gk_out)
    gv[...] = (scaling * nn(k[...], q_round)).astype(BF16)
    write(gv, gv_out)

    for copy in pending:
        copy.wait_send()
    for copy in writes:
        copy.wait()

    @pl.when(c == 1)
    def _():
        send(xsend.at[0], xsend.at[0], disp_send.at[0], disp_recv.at[0], sib).wait_send()
        send(rsend.at[0], rsend.at[0], ret_send.at[0], ret_recv.at[0], sib).wait_send()


def write_out(*refs):
    count = len(refs) // 2
    sem = refs[-1]
    copies = [pltpu.make_async_copy(refs[i], refs[count + i], sem.at[i]) for i in range(count)]
    for copy in copies:
        copy.start()
    for copy in copies:
        copy.wait()


def fused(out_grad, expert_of, counts, w_up, w_down, pre_act, queries, keys, values, w_out):
    n = lax.axis_size("seq")
    m = n // 2
    tok, width = out_grad.shape
    slots = pre_act.shape[0]
    cap = slots // n
    pad = -(-cap // ROWS) * ROWS
    rows = m * pad
    depth, hidden = w_up.shape[1:]
    dim = queries.shape[1]
    pair = 2 * width
    piece = dim // n
    scaling = 1.0 / math.sqrt(dim * tok * n)
    hbm = pl.BlockSpec(memory_space=pltpu.HBM)
    anywhere = pl.BlockSpec(memory_space=pl.ANY)
    dma = pltpu.SemaphoreType.DMA

    def buf(*shape, dtype=BF16):
        return pltpu.VMEM(shape, dtype)

    state = buf(n, piece, dim)
    out = jax.ShapeDtypeStruct((tok, dim), BF16)
    outs = (jax.ShapeDtypeStruct((tok, depth), BF16), out, out, out)
    results = pl.pallas_call(
        functools.partial(kernel, n, pad, scaling),
        out_shape=outs,
        in_specs=[hbm] * 10,
        out_specs=(anywhere,) * 4,
        scratch_shapes=[
            buf(1, tok, dtype=jnp.int32), buf(1, n, dtype=jnp.int32),
            buf(2, depth, hidden), buf(2, hidden, depth), buf(2, slots, hidden), buf(dim, depth),
            buf(tok, dim), buf(tok, dim), buf(tok, dim), buf(2, rows, hidden),
            buf(pair, tok), buf(m, pad, pair), buf(m, pad, depth), buf(m, pad, pair, dtype=F32),
            buf(m, pad, pair), buf(m, pad, pair), buf(m, pad, pair), buf(m, pad, pair),
            buf(tok, pair), buf(tok, pair), buf(tok, depth),
            state, state, state, state, state, state,
            buf(tok, dim), buf(tok, dim), buf(tok, dim),
            dma((10,)), dma((6,)), dma((6,)), dma((m,)), dma((m,)), dma((m,)), dma((m,)),
            dma((m,)), dma((m,)), dma((m,)), dma((m,)), dma((4, n)), dma((4, n)), dma((4,)),
        ],
        compiler_params=pltpu.CompilerParams(
            collective_id=0, has_side_effects=True, vmem_limit_bytes=VMEM_BYTES
        ),
    )(*(pltpu.with_memory_space_constraint(operand, pltpu.HBM) for operand in (
        out_grad.T, expert_of.reshape(1, tok), counts.T, w_up, w_down, pre_act,
        queries, keys, values, w_out,
    )))
    return pl.pallas_call(
        write_out,
        out_shape=outs,
        in_specs=[anywhere] * 4,
        out_specs=(hbm,) * 4,
        scratch_shapes=[dma((4,))],
        compiler_params=pltpu.CompilerParams(vmem_limit_bytes=VMEM_BYTES),
    )(*results)


def step(*arrays):
    n, heads = lax.axis_size("seq"), lax.axis_size("head")
    width, dim = arrays[0].shape[1], arrays[6].shape[1]
    fits = heads == 4 and n % 2 == 0 and dim % (n * ROWS) == 0 and 2 * width % 128 == 0
    return (fused if fits else shards)(*arrays)


def shards(out_grad, expert_of, counts, w_up, w_down, pre_act, queries, keys, values, w_out):
    experts = lax.axis_size("seq")
    tok_rows = out_grad.shape[0]
    slot_count = pre_act.shape[0]
    capacity = slot_count // experts
    head_dim = queries.shape[1]
    scaling = 1.0 / math.sqrt(head_dim * tok_rows * experts)
    full_rows = lax.all_gather(out_grad, "head", axis=1, tiled=True)
    expert_ids = jnp.arange(experts, dtype=jnp.int32)
    onehot = (expert_of[:, None] == expert_ids[None, :]).astype(jnp.int32)
    token_rank = jnp.sum((jnp.cumsum(onehot, axis=0) - 1) * onehot, axis=1)
    slot_of = expert_of * capacity + token_rank
    token_of_slot = (
        jnp.full((experts * capacity,), tok_rows, jnp.int32)
        .at[slot_of]
        .set(jnp.arange(tok_rows, dtype=jnp.int32))
    )
    arrived = counts[:, 0]
    offsets = jnp.cumsum(arrived) - arrived
    arrived_total = jnp.sum(arrived)
    packed_ids = jnp.arange(slot_count, dtype=jnp.int32)
    source = jnp.sum((offsets[None, :] <= packed_ids[:, None]).astype(jnp.int32), axis=1) - 1
    within = packed_ids - offsets[source]
    packed_live = packed_ids < arrived_total
    flat_pos = jnp.where(packed_live, source * capacity + within, experts * capacity)
    down_local = w_down[0]
    up_local = w_up[0]
    padded = jnp.concatenate(
        [full_rows, jnp.zeros((1, full_rows.shape[1]), full_rows.dtype)], axis=0
    )
    received = lax.all_to_all(
        padded[token_of_slot].reshape(experts, capacity, full_rows.shape[1]),
        "seq",
        split_axis=0,
        concat_axis=0,
        tiled=True,
    )
    flat_rows = received.reshape(experts * capacity, received.shape[2])
    padded = jnp.concatenate(
        [flat_rows, jnp.zeros((1, flat_rows.shape[1]), flat_rows.dtype)], axis=0
    )
    middle = jnp.dot(padded[flat_pos], down_local.T, preferred_element_type=jnp.float32)
    mid_grad = jnp.where(pre_act > 0, middle, jnp.zeros_like(middle)).astype(jnp.bfloat16)
    hidden_part = jnp.dot(mid_grad, up_local.T, preferred_element_type=jnp.float32)
    slot_ids = jnp.arange(experts * capacity, dtype=jnp.int32)
    slot_source = slot_ids // capacity
    slot_rank = slot_ids % capacity
    slot_live = slot_rank < arrived[slot_source]
    slot_pos = jnp.where(slot_live, offsets[slot_source] + slot_rank, slot_count)
    share_packed = lax.psum_scatter(
        hidden_part.astype(jnp.bfloat16), "head", scatter_dimension=1, tiled=True
    )
    share_width = share_packed.shape[1]
    padded_grad = jnp.concatenate(
        [share_packed, jnp.zeros((1, share_packed.shape[1]), jnp.bfloat16)], axis=0
    )
    returned = lax.all_to_all(
        padded_grad[slot_pos].reshape(experts, capacity, share_packed.shape[1]),
        "seq",
        split_axis=0,
        concat_axis=0,
        tiled=True,
    )
    share_grad = returned.reshape(experts * capacity, share_width)[slot_of]
    expert_grad = lax.all_gather(share_grad, "head", axis=1, tiled=True)
    grad_hidden = (full_rows.astype(jnp.float32) + expert_grad.astype(jnp.float32)).astype(
        jnp.bfloat16
    )
    head_grad = jnp.dot(grad_hidden, w_out.T, preferred_element_type=jnp.float32).astype(
        jnp.bfloat16
    )
    query_part = jnp.dot(queries.T, head_grad, preferred_element_type=jnp.float32)
    key_state, query_state = lax.psum(
        (jnp.dot(keys.T, values, preferred_element_type=jnp.float32), query_part), "seq"
    )
    key_round = key_state.astype(jnp.bfloat16)
    query_round = query_state.astype(jnp.bfloat16)
    grad_queries = (
        scaling * jnp.dot(head_grad, key_round.T, preferred_element_type=jnp.float32)
    ).astype(jnp.bfloat16)
    grad_keys = (
        scaling * jnp.dot(values, query_round.T, preferred_element_type=jnp.float32)
    ).astype(jnp.bfloat16)
    grad_values = (scaling * jnp.dot(keys, query_round, preferred_element_type=jnp.float32)).astype(
        jnp.bfloat16
    )
    return (grad_hidden, grad_queries, grad_keys, grad_values)


def solution(mesh):
    return jax.shard_map(
        step,
        mesh=mesh,
        in_specs=(
            P("seq", "head"),
            P("seq"),
            P(None, "seq"),
            P("seq", None, "head"),
            P("seq", "head", None),
            P("seq", "head"),
            P("seq", "head"),
            P("seq", "head"),
            P("seq", "head"),
            P("head", None),
        ),
        out_specs=(P("seq", None), P("seq", "head"), P("seq", "head"), P("seq", "head")),
        check_vma=False,
    )
```

```python
import functools
import math

import jax
import jax.numpy as jnp
from jax import lax
from jax.experimental import pallas as pl
from jax.experimental.pallas import tpu as pltpu
from jax.sharding import PartitionSpec as P

MESH = pl.DeviceIdType.MESH
F32 = jnp.float32
BF16 = jnp.bfloat16
ROWS = 16
VMEM_BYTES = 63 * 1024 * 1024


def iota(shape, dim):
    return lax.broadcasted_iota(jnp.int32, shape, dim)


def nn(a, b):
    return jnp.dot(a, b, preferred_element_type=F32)


def nt(a, b):
    return lax.dot_general(a, b, (((1,), (1,)), ((), ())), preferred_element_type=F32)


def kernel(
    n, pad, scaling,
    og_hbm, expert_hbm, counts_hbm, up_hbm, down_hbm, pre_hbm, q_hbm, k_hbm, v_hbm, wout_hbm,
    gh_out, gq_out, gk_out, gv_out,
    expert_of, counts, up, down, pre, wout, q, k, v, mask, grad_t, xsend, x, hsum,
    ysend, yrecv, rsend, ret, eg, eg_in, gh, ks_send, ks_recv, ks, qs_send, qs_recv, qs,
    gq, gk, gv,
    load_sem, one_send, one_recv, disp_send, disp_recv, ax_send, ax_recv,
    hy_send, hy_recv, ret_send, ret_recv, st_send, st_recv, out_sem,
):
    s = lax.axis_index("seq")
    h = lax.axis_index("head")
    c = lax.rem(h, 2)
    y = lax.div(h, 2)
    sib = (s, h + 1 - 2 * c)
    far = (s, lax.rem(h + 2, 4))
    m = n // 2
    width, tok = og_hbm.shape
    pair = 2 * width
    rows = m * pad
    depth = x.shape[2]
    piece = ks.shape[1]
    mine = pl.ds(pl.multiple_of(y * pair, 128), pair)
    other = pl.ds(pl.multiple_of((1 - y) * pair, 128), pair)
    parity = lax.rem(s + c, 2)
    own_rows = pl.ds(pl.multiple_of(c * width, ROWS), width)
    sib_rows = pl.ds(pl.multiple_of((1 - c) * width, ROWS), width)

    def send(src, dst, ssem, rsem, to):
        return pltpu.make_async_remote_copy(
            src_ref=src, dst_ref=dst, send_sem=ssem, recv_sem=rsem, device_id=to, device_id_type=MESH
        )

    barrier = pltpu.get_barrier_semaphore()
    peers = [lax.rem(s + d, n) for d in range(1, n)]
    for p in peers:
        pl.semaphore_signal(barrier, inc=1, device_id=(p, h), device_id_type=MESH)
    for to in (sib, far):
        pl.semaphore_signal(barrier, inc=1, device_id=to, device_id_type=MESH)
    loads = {}
    for i, (name, src, dst) in enumerate((
        ("expert", expert_hbm, expert_of), ("grad", og_hbm, grad_t.at[own_rows]),
        ("k", k_hbm, k), ("v", v_hbm, v), ("counts", counts_hbm, counts),
        ("pre", pre_hbm, pre.at[0]), ("down", down_hbm.at[0], down.at[0]),
        ("up", up_hbm.at[0], up.at[0]), ("wout", wout_hbm, wout),
        ("q", q_hbm, q),
    )):
        loads[name] = pltpu.make_async_copy(src, dst, load_sem.at[i])
        loads[name].start()

    pl.semaphore_wait(barrier, n + 1)
    pending = []

    def start(copy):
        copy.start()
        pending.append(copy)
        return copy

    loads["grad"].wait()
    spot = grad_t.at[own_rows]
    start(send(spot, spot, one_send.at[0], one_recv.at[0], sib))
    swaps = []
    for i, (name, both) in enumerate((("pre", pre), ("down", down), ("up", up))):
        loads[name].wait()
        swaps.append(start(send(both.at[0], both.at[1], one_send.at[3 + i], one_recv.at[3 + i], sib)))

    loads["expert"].wait()
    e_row = expert_of[...]
    eye = iota((tok, tok), 0) == iota((tok, tok), 1)
    e_col = jnp.sum(jnp.where(eye, e_row, 0), axis=1, keepdims=True)
    same = (e_col == e_row).astype(jnp.int32)
    below = iota((tok, tok), 0) < iota((tok, tok), 1)
    rank_row = jnp.sum(jnp.where(below, same, 0), axis=0, keepdims=True)
    live_row = lax.rem(e_row, 2) == parity
    slot_row = jnp.where(live_row, lax.div(e_row, 2) * pad + rank_row, -1)
    scatter = (iota((rows, tok), 0) == slot_row).astype(BF16)

    spot = grad_t.at[sib_rows]
    send(spot, spot, one_send.at[0], one_recv.at[0], sib).wait_recv()
    blocks = nt(scatter, grad_t[...]).astype(BF16)
    for i in range(m):
        xsend[i] = blocks[i * pad : (i + 1) * pad]
    turns = [*range(1, m), 0]
    order = [(j, lax.rem(s + c + 2 * j, n)) for j in turns]
    for j, p in order:
        copy = send(
            xsend.at[lax.div(p, 2)], x.at[lax.div(s, 2), :, mine],
            disp_send.at[j], disp_recv.at[lax.div(s, 2)], (p, h),
        )
        if j == 0:
            pl.when(c == 1)(copy.start)

            @pl.when(c == 0)
            def _():
                x[lax.div(s, 2), :, mine] = xsend[lax.div(s, 2)]
        else:
            start(copy)

    loads["counts"].wait()
    slot = iota((rows, 1), 0)
    source = 2 * lax.div(slot, pad) + parity
    before = iota((rows, n), 1) < source
    packed = jnp.sum(jnp.where(before, counts[...], 0), axis=1, keepdims=True) + lax.rem(slot, pad)
    unpack = (iota((rows, pre.shape[1]), 1) == packed).astype(BF16)
    mask[0] = nn(unpack, pre[0]).astype(BF16)

    for j, p in order:
        i = lax.div(p, 2)
        spot = x.at[i, :, mine]
        copy = send(spot, spot, disp_send.at[j], disp_recv.at[i], (p, h))
        if j == 0:
            pl.when(c == 1)(copy.wait_recv)
        else:
            copy.wait_recv()
        start(send(spot, spot, ax_send.at[j], ax_recv.at[j], far))

    loads["k"].wait()
    loads["v"].wait()
    ks_part = nn(k[...].T, v[...]).astype(BF16)
    for p in range(n):
        ks_send[p] = ks_part[p * piece : (p + 1) * piece]

    def state_scatter(at, source, dest):
        for d, p in enumerate(peers):
            start(send(source.at[p], dest.at[s], st_send.at[at, d], st_recv.at[at, s], (p, h)))
        dest[s] = source[s]

    def state_sum(at, dest, total):
        for p in peers:
            send(dest.at[p], dest.at[p], st_send.at[at, 0], st_recv.at[at, p], (p, h)).wait_recv()
        acc = dest[0].astype(F32)
        for p in range(1, n):
            acc = acc + dest[p].astype(F32)
        total[s] = acc.astype(BF16)
        for d, p in enumerate(peers):
            start(send(
                total.at[s], total.at[s], st_send.at[at + 1, d], st_recv.at[at + 1, s], (p, h)
            ))

    def state_wait(at, total):
        for p in peers:
            send(total.at[p], total.at[p], st_send.at[at, 0], st_recv.at[at, p], (p, h)).wait_recv()

    state_scatter(0, ks_send, ks_recv)

    swaps[0].wait_recv()
    mask[1] = nn(unpack, pre[1]).astype(BF16)
    swaps[1].wait_recv()
    ready = x[:, :, mine].reshape(rows, pair)
    middle = [nt(ready, down[u, :, mine]) for u in range(2)]
    swaps[2].wait_recv()
    for j, p in order:
        spot = x.at[lax.div(p, 2), :, other]
        send(spot, spot, ax_send.at[j], ax_recv.at[j], far).wait_recv()
    ready = x[:, :, other].reshape(rows, pair)
    mid = [
        jnp.where(mask[u] > 0, middle[u] + nt(ready, down[u, :, other]), 0.0).astype(BF16)
        for u in range(2)
    ]
    ysend[...] = (nt(mid[0], up[0, other, :]) + nt(mid[1], up[1, other, :])).astype(BF16).reshape(
        m, pad, pair
    )
    for j, p in order:
        i = lax.div(p, 2)
        start(send(ysend.at[i], yrecv.at[i], hy_send.at[j], hy_recv.at[j], far))
    hsum[...] = (nt(mid[0], up[0, mine, :]) + nt(mid[1], up[1, mine, :])).reshape(m, pad, pair)
    state_sum(0, ks_recv, ks)

    for j, p in order:
        i = lax.div(p, 2)
        spot = yrecv.at[i]
        send(spot, spot, hy_send.at[j], hy_recv.at[j], far).wait_recv()
        rsend[i] = (hsum[i] + yrecv[i].astype(F32)).astype(BF16)
        copy = send(
            rsend.at[i], ret.at[lax.div(s, 2)], ret_send.at[j], ret_recv.at[lax.div(s, 2)], (p, h)
        )
        if j == 0:
            pl.when(c == 1)(copy.start)

            @pl.when(c == 0)
            def _():
                ret[lax.div(s, 2)] = rsend[lax.div(s, 2)]
        else:
            start(copy)
    above = iota((tok, tok), 1) < iota((tok, tok), 0)
    rank_col = jnp.sum(jnp.where(above, same, 0), axis=1, keepdims=True)
    live_col = lax.rem(e_col, 2) == parity
    slot_col = jnp.where(live_col, lax.div(e_col, 2) * pad + rank_col, -1)
    combine = (iota((tok, rows), 1) == slot_col).astype(BF16)
    own = grad_t[...].astype(F32).T
    loads["wout"].wait()
    loads["q"].wait()
    q_t = q[...].T
    for j, p in order:
        i = lax.div(p, 2)
        copy = send(ret.at[i], ret.at[i], ret_send.at[j], ret_recv.at[i], (p, h))
        if j == 0:
            pl.when(c == 1)(copy.wait_recv)
        else:
            copy.wait_recv()
    share = nn(combine, ret[...].reshape(rows, pair))
    eg[...] = share.astype(BF16)
    start(send(eg, eg_in, one_send.at[1], one_recv.at[1], sib))
    own = own + share
    send(eg, eg_in, one_send.at[1], one_recv.at[1], sib).wait_recv()
    half = (own + eg_in[...].astype(F32)).astype(BF16)
    gh[:, mine] = half
    spot = gh.at[:, mine]
    start(send(spot, spot, one_send.at[2], one_recv.at[2], far))
    head_part = nt(half, wout[:, mine])
    state_wait(1, ks)
    spot = gh.at[:, other]
    send(spot, spot, one_send.at[2], one_recv.at[2], far).wait_recv()
    head_grad = (head_part + nt(gh[:, other], wout[:, other])).astype(BF16)
    qs_part = nn(q_t, head_grad).astype(BF16)
    for p in range(n):
        qs_send[p] = qs_part[p * piece : (p + 1) * piece]
    state_scatter(2, qs_send, qs_recv)
    writes = []

    def write(src, dst):
        writes.append(pltpu.make_async_copy(src, dst, out_sem.at[len(writes)]))
        writes[-1].start()

    write(gh, gh_out)
    dim = n * piece
    gq[...] = (scaling * nt(head_grad, ks[...].reshape(dim, dim))).astype(BF16)
    write(gq, gq_out)
    state_sum(2, qs_recv, qs)
    state_wait(3, qs)
    q_round = qs[...].reshape(dim, dim)
    gk[...] = (scaling * nt(v[...], q_round)).astype(BF16)
    write(gk, gk_out)
    gv[...] = (scaling * nn(k[...], q_round)).astype(BF16)
    write(gv, gv_out)

    for copy in pending:
        copy.wait_send()
    for copy in writes:
        copy.wait()

    @pl.when(c == 1)
    def _():
        send(xsend.at[0], xsend.at[0], disp_send.at[0], disp_recv.at[0], sib).wait_send()
        send(rsend.at[0], rsend.at[0], ret_send.at[0], ret_recv.at[0], sib).wait_send()


def write_out(*refs):
    sources, dests, rooms, (come, go) = refs[:4], refs[4:8], refs[8:12], refs[12:]
    ins = [pltpu.make_async_copy(a, b, come.at[i]) for i, (a, b) in enumerate(zip(sources, rooms))]
    outs = [pltpu.make_async_copy(a, b, go.at[i]) for i, (a, b) in enumerate(zip(rooms, dests))]
    for copy in ins:
        copy.start()
    for first, second in zip(ins, outs):
        first.wait()
        second.start()
    for copy in outs:
        copy.wait()


def fused(out_grad, expert_of, counts, w_up, w_down, pre_act, queries, keys, values, w_out):
    n = lax.axis_size("seq")
    m = n // 2
    tok, width = out_grad.shape
    slots = pre_act.shape[0]
    cap = slots // n
    pad = -(-cap // ROWS) * ROWS
    rows = m * pad
    depth, hidden = w_up.shape[1:]
    dim = queries.shape[1]
    pair = 2 * width
    piece = dim // n
    scaling = 1.0 / math.sqrt(dim * tok * n)
    hbm = pl.BlockSpec(memory_space=pltpu.HBM)
    anywhere = pl.BlockSpec(memory_space=pl.ANY)
    dma = pltpu.SemaphoreType.DMA

    def buf(*shape, dtype=BF16):
        return pltpu.VMEM(shape, dtype)

    state = buf(n, piece, dim)
    out = jax.ShapeDtypeStruct((tok, dim), BF16)
    outs = (jax.ShapeDtypeStruct((tok, depth), BF16), out, out, out)
    results = pl.pallas_call(
        functools.partial(kernel, n, pad, scaling),
        out_shape=outs,
        in_specs=[hbm] * 10,
        out_specs=(anywhere,) * 4,
        scratch_shapes=[
            buf(1, tok, dtype=jnp.int32), buf(1, n, dtype=jnp.int32),
            buf(2, depth, hidden), buf(2, hidden, depth), buf(2, slots, hidden), buf(dim, depth),
            buf(tok, dim), buf(tok, dim), buf(tok, dim), buf(2, rows, hidden),
            buf(pair, tok), buf(m, pad, pair), buf(m, pad, depth), buf(m, pad, pair, dtype=F32),
            buf(m, pad, pair), buf(m, pad, pair), buf(m, pad, pair), buf(m, pad, pair),
            buf(tok, pair), buf(tok, pair), buf(tok, depth),
            state, state, state, state, state, state,
            buf(tok, dim), buf(tok, dim), buf(tok, dim),
            dma((10,)), dma((6,)), dma((6,)), dma((m,)), dma((m,)), dma((m,)), dma((m,)),
            dma((m,)), dma((m,)), dma((m,)), dma((m,)), dma((4, n)), dma((4, n)), dma((4,)),
        ],
        compiler_params=pltpu.CompilerParams(
            collective_id=0, has_side_effects=True, vmem_limit_bytes=VMEM_BYTES
        ),
    )(*(pltpu.with_memory_space_constraint(operand, pltpu.HBM) for operand in (
        out_grad.T, expert_of.reshape(1, tok), counts.T, w_up, w_down, pre_act,
        queries, keys, values, w_out,
    )))
    return pl.pallas_call(
        write_out,
        out_shape=outs,
        in_specs=[anywhere] * 4,
        out_specs=(hbm,) * 4,
        scratch_shapes=[*(buf(*a.shape) for a in outs), dma((4,)), dma((4,))],
        compiler_params=pltpu.CompilerParams(vmem_limit_bytes=VMEM_BYTES),
    )(*results)


def step(*arrays):
    n, heads = lax.axis_size("seq"), lax.axis_size("head")
    width, dim = arrays[0].shape[1], arrays[6].shape[1]
    fits = heads == 4 and n % 2 == 0 and dim % (n * ROWS) == 0 and 2 * width % 128 == 0
    return (fused if fits else shards)(*arrays)


def shards(out_grad, expert_of, counts, w_up, w_down, pre_act, queries, keys, values, w_out):
    experts = lax.axis_size("seq")
    tok_rows = out_grad.shape[0]
    slot_count = pre_act.shape[0]
    capacity = slot_count // experts
    head_dim = queries.shape[1]
    scaling = 1.0 / math.sqrt(head_dim * tok_rows * experts)
    full_rows = lax.all_gather(out_grad, "head", axis=1, tiled=True)
    expert_ids = jnp.arange(experts, dtype=jnp.int32)
    onehot = (expert_of[:, None] == expert_ids[None, :]).astype(jnp.int32)
    token_rank = jnp.sum((jnp.cumsum(onehot, axis=0) - 1) * onehot, axis=1)
    slot_of = expert_of * capacity + token_rank
    token_of_slot = (
        jnp.full((experts * capacity,), tok_rows, jnp.int32)
        .at[slot_of]
        .set(jnp.arange(tok_rows, dtype=jnp.int32))
    )
    arrived = counts[:, 0]
    offsets = jnp.cumsum(arrived) - arrived
    arrived_total = jnp.sum(arrived)
    packed_ids = jnp.arange(slot_count, dtype=jnp.int32)
    source = jnp.sum((offsets[None, :] <= packed_ids[:, None]).astype(jnp.int32), axis=1) - 1
    within = packed_ids - offsets[source]
    packed_live = packed_ids < arrived_total
    flat_pos = jnp.where(packed_live, source * capacity + within, experts * capacity)
    down_local = w_down[0]
    up_local = w_up[0]
    padded = jnp.concatenate(
        [full_rows, jnp.zeros((1, full_rows.shape[1]), full_rows.dtype)], axis=0
    )
    received = lax.all_to_all(
        padded[token_of_slot].reshape(experts, capacity, full_rows.shape[1]),
        "seq",
        split_axis=0,
        concat_axis=0,
        tiled=True,
    )
    flat_rows = received.reshape(experts * capacity, received.shape[2])
    padded = jnp.concatenate(
        [flat_rows, jnp.zeros((1, flat_rows.shape[1]), flat_rows.dtype)], axis=0
    )
    middle = jnp.dot(padded[flat_pos], down_local.T, preferred_element_type=jnp.float32)
    mid_grad = jnp.where(pre_act > 0, middle, jnp.zeros_like(middle)).astype(jnp.bfloat16)
    hidden_part = jnp.dot(mid_grad, up_local.T, preferred_element_type=jnp.float32)
    slot_ids = jnp.arange(experts * capacity, dtype=jnp.int32)
    slot_source = slot_ids // capacity
    slot_rank = slot_ids % capacity
    slot_live = slot_rank < arrived[slot_source]
    slot_pos = jnp.where(slot_live, offsets[slot_source] + slot_rank, slot_count)
    share_packed = lax.psum_scatter(
        hidden_part.astype(jnp.bfloat16), "head", scatter_dimension=1, tiled=True
    )
    share_width = share_packed.shape[1]
    padded_grad = jnp.concatenate(
        [share_packed, jnp.zeros((1, share_packed.shape[1]), jnp.bfloat16)], axis=0
    )
    returned = lax.all_to_all(
        padded_grad[slot_pos].reshape(experts, capacity, share_packed.shape[1]),
        "seq",
        split_axis=0,
        concat_axis=0,
        tiled=True,
    )
    share_grad = returned.reshape(experts * capacity, share_width)[slot_of]
    expert_grad = lax.all_gather(share_grad, "head", axis=1, tiled=True)
    grad_hidden = (full_rows.astype(jnp.float32) + expert_grad.astype(jnp.float32)).astype(
        jnp.bfloat16
    )
    head_grad = jnp.dot(grad_hidden, w_out.T, preferred_element_type=jnp.float32).astype(
        jnp.bfloat16
    )
    query_part = jnp.dot(queries.T, head_grad, preferred_element_type=jnp.float32)
    key_state, query_state = lax.psum(
        (jnp.dot(keys.T, values, preferred_element_type=jnp.float32), query_part), "seq"
    )
    key_round = key_state.astype(jnp.bfloat16)
    query_round = query_state.astype(jnp.bfloat16)
    grad_queries = (
        scaling * jnp.dot(head_grad, key_round.T, preferred_element_type=jnp.float32)
    ).astype(jnp.bfloat16)
    grad_keys = (
        scaling * jnp.dot(values, query_round.T, preferred_element_type=jnp.float32)
    ).astype(jnp.bfloat16)
    grad_values = (scaling * jnp.dot(keys, query_round, preferred_element_type=jnp.float32)).astype(
        jnp.bfloat16
    )
    return (grad_hidden, grad_queries, grad_keys, grad_values)


def solution(mesh):
    return jax.shard_map(
        step,
        mesh=mesh,
        in_specs=(
            P("seq", "head"),
            P("seq"),
            P(None, "seq"),
            P("seq", None, "head"),
            P("seq", "head", None),
            P("seq", "head"),
            P("seq", "head"),
            P("seq", "head"),
            P("seq", "head"),
            P("head", None),
        ),
        out_specs=(P("seq", None), P("seq", "head"), P("seq", "head"), P("seq", "head")),
        check_vma=False,
    )
```

```python
import functools
import math

import jax
import jax.numpy as jnp
from jax import lax
from jax.experimental import pallas as pl
from jax.experimental.pallas import tpu as pltpu
from jax.sharding import PartitionSpec as P

MESH = pl.DeviceIdType.MESH
F32 = jnp.float32
BF16 = jnp.bfloat16
ROWS = 16
VMEM_BYTES = 32 * 1024 * 1024


def iota(shape, dim):
    return lax.broadcasted_iota(jnp.int32, shape, dim)


def nn(a, b):
    return jnp.dot(a, b, preferred_element_type=F32)


def nt(a, b):
    return lax.dot_general(a, b, (((1,), (1,)), ((), ())), preferred_element_type=F32)


def kernel(
    n, pad, scaling,
    og_hbm, expert_hbm, counts_hbm, up_hbm, down_hbm, pre_hbm, q_hbm, k_hbm, v_hbm, wout_hbm,
    gh, gq, gk, gv,
    expert_of, counts, up, down, pre, wout, q, k, v, mask, grad_t, xsend, x, hsum,
    ysend, yrecv, rsend, ret, part, part_in, grads, wall, head_send, head_recv,
    ks_send, ks_recv, ks, qs_send, qs_recv, qs,
    load_sem, one_send, one_recv, disp_send, disp_recv, ax_send, ax_recv,
    hy_send, hy_recv, ret_send, ret_recv, st_send, st_recv, wall_send, wall_recv, head_ssem, head_rsem,
):
    s = lax.axis_index("seq")
    h = lax.axis_index("head")
    c = lax.rem(h, 2)
    y = lax.div(h, 2)
    sib = (s, h + 1 - 2 * c)
    far = (s, lax.rem(h + 2, 4))
    diag = (s, lax.rem(sib[1] + 2, 4))
    m = n // 2
    width, tok = og_hbm.shape
    pair = 2 * width
    rows = m * pad
    depth = x.shape[2]
    piece = ks.shape[1]
    mine = pl.ds(pl.multiple_of(y * pair, 128), pair)
    other = pl.ds(pl.multiple_of((1 - y) * pair, 128), pair)
    parity = lax.rem(s + c, 2)
    own_rows = pl.ds(pl.multiple_of(c * width, ROWS), width)
    sib_rows = pl.ds(pl.multiple_of((1 - c) * width, ROWS), width)

    def send(src, dst, ssem, rsem, to):
        return pltpu.make_async_remote_copy(
            src_ref=src, dst_ref=dst, send_sem=ssem, recv_sem=rsem, device_id=to, device_id_type=MESH
        )

    barrier = pltpu.get_barrier_semaphore()
    peers = [lax.rem(s + d, n) for d in range(1, n)]
    for p in peers:
        pl.semaphore_signal(barrier, inc=1, device_id=(p, h), device_id_type=MESH)
    for to in (sib, far, diag):
        pl.semaphore_signal(barrier, inc=1, device_id=to, device_id_type=MESH)
    loads = {}
    for i, (name, src, dst) in enumerate((
        ("expert", expert_hbm, expert_of), ("grad", og_hbm, grad_t.at[own_rows]),
        ("k", k_hbm, k), ("v", v_hbm, v), ("counts", counts_hbm, counts),
        ("pre", pre_hbm, pre.at[0]), ("down", down_hbm.at[0], down.at[0]),
        ("up", up_hbm.at[0], up.at[0]), ("wout", wout_hbm, wout),
        ("q", q_hbm, q),
    )):
        loads[name] = pltpu.make_async_copy(src, dst, load_sem.at[i])
        loads[name].start()

    pl.semaphore_wait(barrier, n + 2)
    pending = []

    def start(copy):
        copy.start()
        pending.append(copy)
        return copy

    loads["grad"].wait()
    spot = grad_t.at[own_rows]
    start(send(spot, spot, one_send.at[0], one_recv.at[0], sib))
    swaps = []
    for i, (name, both) in enumerate((("pre", pre), ("down", down), ("up", up))):
        loads[name].wait()
        swaps.append(start(send(both.at[0], both.at[1], one_send.at[3 + i], one_recv.at[3 + i], sib)))

    loads["wout"].wait()
    wall[h] = wout[:, mine]
    start(send(wout.at[:, other], wall.at[h], wall_send.at[0], wall_recv.at[0], far))
    start(send(wout.at[:, mine], wall.at[h], wall_send.at[1], wall_recv.at[1], sib))

    loads["expert"].wait()
    e_row = expert_of[...]
    eye = iota((tok, tok), 0) == iota((tok, tok), 1)
    e_col = jnp.sum(jnp.where(eye, e_row, 0), axis=1, keepdims=True)
    same = (e_col == e_row).astype(jnp.int32)
    below = iota((tok, tok), 0) < iota((tok, tok), 1)
    rank_row = jnp.sum(jnp.where(below, same, 0), axis=0, keepdims=True)
    live_row = lax.rem(e_row, 2) == parity
    slot_row = jnp.where(live_row, lax.div(e_row, 2) * pad + rank_row, -1)
    scatter = (iota((rows, tok), 0) == slot_row).astype(BF16)

    spot = grad_t.at[sib_rows]
    send(spot, spot, one_send.at[0], one_recv.at[0], sib).wait_recv()
    blocks = nt(scatter, grad_t[...]).astype(BF16)
    for i in range(m):
        xsend[i] = blocks[i * pad : (i + 1) * pad]
    turns = [*range(1, m), 0]
    order = [(j, lax.rem(s + c + 2 * j, n)) for j in turns]
    for j, p in order:
        copy = send(
            xsend.at[lax.div(p, 2)], x.at[lax.div(s, 2), :, mine],
            disp_send.at[j], disp_recv.at[lax.div(s, 2)], (p, h),
        )
        if j == 0:
            pl.when(c == 1)(copy.start)

            @pl.when(c == 0)
            def _():
                x[lax.div(s, 2), :, mine] = xsend[lax.div(s, 2)]
        else:
            start(copy)

    loads["counts"].wait()
    slot = iota((rows, 1), 0)
    source = 2 * lax.div(slot, pad) + parity
    before = iota((rows, n), 1) < source
    packed = jnp.sum(jnp.where(before, counts[...], 0), axis=1, keepdims=True) + lax.rem(slot, pad)
    unpack = (iota((rows, pre.shape[1]), 1) == packed).astype(BF16)
    mask[0] = nn(unpack, pre[0]).astype(BF16)

    near = [(j, lax.rem(s + c + 2 * j, n)) for j in sorted(range(m), key=lambda j: min(j, m - j))]
    for j, p in near:
        i = lax.div(p, 2)
        spot = x.at[i, :, mine]
        copy = send(spot, spot, disp_send.at[j], disp_recv.at[i], (p, h))
        if j == 0:
            pl.when(c == 1)(copy.wait_recv)
        else:
            copy.wait_recv()
        start(send(spot, spot, ax_send.at[j], ax_recv.at[j], far))

    spot = wall.at[far[1]]
    send(spot, spot, wall_send.at[0], wall_recv.at[0], far).wait_recv()
    start(send(spot, spot, wall_send.at[2], wall_recv.at[2], sib))

    loads["k"].wait()
    loads["v"].wait()
    ks_part = nn(k[...].T, v[...]).astype(BF16)
    for p in range(n):
        ks_send[p] = ks_part[p * piece : (p + 1) * piece]

    def state_scatter(at, source, dest):
        for d, p in enumerate(peers):
            start(send(source.at[p], dest.at[s], st_send.at[at, d], st_recv.at[at, s], (p, h)))
        dest[s] = source[s]

    def state_sum(at, dest, total):
        for p in peers:
            send(dest.at[p], dest.at[p], st_send.at[at, 0], st_recv.at[at, p], (p, h)).wait_recv()
        acc = dest[0].astype(F32)
        for p in range(1, n):
            acc = acc + dest[p].astype(F32)
        total[s] = acc.astype(BF16)
        for d, p in enumerate(peers):
            start(send(
                total.at[s], total.at[s], st_send.at[at + 1, d], st_recv.at[at + 1, s], (p, h)
            ))

    def state_wait(at, total):
        for p in peers:
            send(total.at[p], total.at[p], st_send.at[at, 0], st_recv.at[at, p], (p, h)).wait_recv()

    state_scatter(0, ks_send, ks_recv)

    swaps[0].wait_recv()
    mask[1] = nn(unpack, pre[1]).astype(BF16)
    swaps[1].wait_recv()
    ready = x[:, :, mine].reshape(rows, pair)
    middle = [nt(ready, down[u, :, mine]) for u in range(2)]
    swaps[2].wait_recv()
    for j, p in near:
        spot = x.at[lax.div(p, 2), :, other]
        send(spot, spot, ax_send.at[j], ax_recv.at[j], far).wait_recv()
    ready = x[:, :, other].reshape(rows, pair)
    mid = [
        jnp.where(mask[u] > 0, middle[u] + nt(ready, down[u, :, other]), 0.0).astype(BF16)
        for u in range(2)
    ]
    ysend[...] = (nt(mid[0], up[0, other, :]) + nt(mid[1], up[1, other, :])).astype(BF16).reshape(
        m, pad, pair
    )
    for j, p in order:
        i = lax.div(p, 2)
        start(send(ysend.at[i], yrecv.at[i], hy_send.at[j], hy_recv.at[j], far))
    hsum[...] = (nt(mid[0], up[0, mine, :]) + nt(mid[1], up[1, mine, :])).reshape(m, pad, pair)
    state_sum(0, ks_recv, ks)

    for j, p in order:
        i = lax.div(p, 2)
        spot = yrecv.at[i]
        send(spot, spot, hy_send.at[j], hy_recv.at[j], far).wait_recv()
        rsend[i] = (hsum[i] + yrecv[i].astype(F32)).astype(BF16)
        copy = send(
            rsend.at[i], ret.at[lax.div(s, 2)], ret_send.at[j], ret_recv.at[lax.div(s, 2)], (p, h)
        )
        if j == 0:
            pl.when(c == 1)(copy.start)

            @pl.when(c == 0)
            def _():
                ret[lax.div(s, 2)] = rsend[lax.div(s, 2)]
        else:
            start(copy)
    above = iota((tok, tok), 1) < iota((tok, tok), 0)
    rank_col = jnp.sum(jnp.where(above, same, 0), axis=1, keepdims=True)
    live_col = lax.rem(e_col, 2) == parity
    slot_col = jnp.where(live_col, lax.div(e_col, 2) * pad + rank_col, -1)
    combine = (iota((tok, rows), 1) == slot_col).astype(BF16)
    own = jnp.where(live_col, grad_t[...].astype(F32).T, 0.0)
    loads["q"].wait()
    q_t = q[...].T
    spot = wall.at[sib[1]]
    send(spot, spot, wall_send.at[1], wall_recv.at[1], sib).wait_recv()
    spot = wall.at[diag[1]]
    send(spot, spot, wall_send.at[2], wall_recv.at[2], sib).wait_recv()
    state_wait(1, ks)
    for j, p in near:
        i = lax.div(p, 2)
        copy = send(ret.at[i], ret.at[i], ret_send.at[j], ret_recv.at[i], (p, h))
        if j == 0:
            pl.when(c == 1)(copy.wait_recv)
        else:
            copy.wait_recv()
    half = (own + nn(combine, ret[...].reshape(rows, pair))).astype(BF16)
    for i, to in enumerate((diag, far, sib)):
        head_send[i] = nt(half, wall[to[1]]).astype(BF16)
        start(send(head_send.at[i], head_recv.at[i], head_ssem.at[i], head_rsem.at[i], to))
    part[...] = half
    start(send(part, part_in, one_send.at[1], one_recv.at[1], sib))
    head_sum = nt(half, wall[h])
    for i, to in ((2, sib), (1, far), (0, diag)):
        spot = head_recv.at[i]
        send(spot, spot, head_ssem.at[i], head_rsem.at[i], to).wait_recv()
        head_sum = head_sum + head_recv[i].astype(F32)
    head_grad = head_sum.astype(BF16)
    qs_part = nn(q_t, head_grad).astype(BF16)
    for p in range(n):
        qs_send[p] = qs_part[p * piece : (p + 1) * piece]
    state_scatter(2, qs_send, qs_recv)
    send(part, part_in, one_send.at[1], one_recv.at[1], sib).wait_recv()
    grads[:, mine] = part[...] + part_in[...]
    spot = grads.at[:, mine]
    start(send(spot, spot, one_send.at[2], one_recv.at[2], far))
    dim = n * piece
    gq[...] = (scaling * nt(head_grad, ks[...].reshape(dim, dim))).astype(BF16)
    state_sum(2, qs_recv, qs)
    spot = grads.at[:, other]
    send(spot, spot, one_send.at[2], one_recv.at[2], far).wait_recv()
    gh[...] = grads[...]
    state_wait(3, qs)
    q_round = qs[...].reshape(dim, dim)
    gk[...] = (scaling * nt(v[...], q_round)).astype(BF16)
    gv[...] = (scaling * nn(k[...], q_round)).astype(BF16)

    for copy in pending:
        copy.wait_send()

    @pl.when(c == 1)
    def _():
        send(xsend.at[0], xsend.at[0], disp_send.at[0], disp_recv.at[0], sib).wait_send()
        send(rsend.at[0], rsend.at[0], ret_send.at[0], ret_recv.at[0], sib).wait_send()


def write_out(*refs):
    count = len(refs) // 2
    sem = refs[-1]
    copies = [pltpu.make_async_copy(refs[i], refs[count + i], sem.at[i]) for i in range(count)]
    for copy in copies:
        copy.start()
    for copy in copies:
        copy.wait()


def fused(out_grad, expert_of, counts, w_up, w_down, pre_act, queries, keys, values, w_out):
    n = lax.axis_size("seq")
    m = n // 2
    tok, width = out_grad.shape
    slots = pre_act.shape[0]
    cap = slots // n
    pad = -(-cap // ROWS) * ROWS
    rows = m * pad
    depth, hidden = w_up.shape[1:]
    dim = queries.shape[1]
    pair = 2 * width
    piece = dim // n
    scaling = 1.0 / math.sqrt(dim * tok * n)
    hbm = pl.BlockSpec(memory_space=pltpu.HBM)
    vmem = pl.BlockSpec(memory_space=pltpu.VMEM)
    dma = pltpu.SemaphoreType.DMA

    def buf(*shape, dtype=BF16):
        return pltpu.VMEM(shape, dtype)

    state = buf(n, piece, dim)
    out = jax.ShapeDtypeStruct((tok, dim), BF16)
    outs = (jax.ShapeDtypeStruct((tok, depth), BF16), out, out, out)
    results = pl.pallas_call(
        functools.partial(kernel, n, pad, scaling),
        out_shape=outs,
        in_specs=[hbm] * 10,
        out_specs=(vmem,) * 4,
        scratch_shapes=[
            buf(1, tok, dtype=jnp.int32), buf(1, n, dtype=jnp.int32),
            buf(2, depth, hidden), buf(2, hidden, depth), buf(2, slots, hidden), buf(dim, depth),
            buf(tok, dim), buf(tok, dim), buf(tok, dim), buf(2, rows, hidden),
            buf(pair, tok), buf(m, pad, pair), buf(m, pad, depth), buf(m, pad, pair, dtype=F32),
            buf(m, pad, pair), buf(m, pad, pair), buf(m, pad, pair), buf(m, pad, pair),
            buf(tok, pair), buf(tok, pair), buf(tok, depth),
            buf(4, dim, pair), buf(3, tok, dim), buf(3, tok, dim),
            state, state, state, state, state, state,
            dma((10,)), dma((6,)), dma((6,)), dma((m,)), dma((m,)), dma((m,)), dma((m,)),
            dma((m,)), dma((m,)), dma((m,)), dma((m,)), dma((4, n)), dma((4, n)), dma((3,)), dma((3,)),
            dma((3,)), dma((3,)),
        ],
        compiler_params=pltpu.CompilerParams(
            collective_id=0, has_side_effects=True, vmem_limit_bytes=VMEM_BYTES
        ),
    )(*(pltpu.with_memory_space_constraint(operand, pltpu.HBM) for operand in (
        out_grad.T, expert_of.reshape(1, tok), counts.T, w_up, w_down, pre_act,
        queries, keys, values, w_out,
    )))
    return pl.pallas_call(
        write_out,
        out_shape=outs,
        in_specs=[vmem] * 4,
        out_specs=(hbm,) * 4,
        scratch_shapes=[dma((4,))],
        compiler_params=pltpu.CompilerParams(vmem_limit_bytes=VMEM_BYTES // 8),
    )(*results)


def step(*arrays):
    n, heads = lax.axis_size("seq"), lax.axis_size("head")
    width, dim = arrays[0].shape[1], arrays[6].shape[1]
    fits = heads == 4 and n % 2 == 0 and dim % (n * ROWS) == 0 and 2 * width % 128 == 0
    return (fused if fits else shards)(*arrays)


def shards(out_grad, expert_of, counts, w_up, w_down, pre_act, queries, keys, values, w_out):
    experts = lax.axis_size("seq")
    tok_rows = out_grad.shape[0]
    slot_count = pre_act.shape[0]
    capacity = slot_count // experts
    head_dim = queries.shape[1]
    scaling = 1.0 / math.sqrt(head_dim * tok_rows * experts)
    full_rows = lax.all_gather(out_grad, "head", axis=1, tiled=True)
    expert_ids = jnp.arange(experts, dtype=jnp.int32)
    onehot = (expert_of[:, None] == expert_ids[None, :]).astype(jnp.int32)
    token_rank = jnp.sum((jnp.cumsum(onehot, axis=0) - 1) * onehot, axis=1)
    slot_of = expert_of * capacity + token_rank
    token_of_slot = (
        jnp.full((experts * capacity,), tok_rows, jnp.int32)
        .at[slot_of]
        .set(jnp.arange(tok_rows, dtype=jnp.int32))
    )
    arrived = counts[:, 0]
    offsets = jnp.cumsum(arrived) - arrived
    arrived_total = jnp.sum(arrived)
    packed_ids = jnp.arange(slot_count, dtype=jnp.int32)
    source = jnp.sum((offsets[None, :] <= packed_ids[:, None]).astype(jnp.int32), axis=1) - 1
    within = packed_ids - offsets[source]
    packed_live = packed_ids < arrived_total
    flat_pos = jnp.where(packed_live, source * capacity + within, experts * capacity)
    down_local = w_down[0]
    up_local = w_up[0]
    padded = jnp.concatenate(
        [full_rows, jnp.zeros((1, full_rows.shape[1]), full_rows.dtype)], axis=0
    )
    received = lax.all_to_all(
        padded[token_of_slot].reshape(experts, capacity, full_rows.shape[1]),
        "seq",
        split_axis=0,
        concat_axis=0,
        tiled=True,
    )
    flat_rows = received.reshape(experts * capacity, received.shape[2])
    padded = jnp.concatenate(
        [flat_rows, jnp.zeros((1, flat_rows.shape[1]), flat_rows.dtype)], axis=0
    )
    middle = jnp.dot(padded[flat_pos], down_local.T, preferred_element_type=jnp.float32)
    mid_grad = jnp.where(pre_act > 0, middle, jnp.zeros_like(middle)).astype(jnp.bfloat16)
    hidden_part = jnp.dot(mid_grad, up_local.T, preferred_element_type=jnp.float32)
    slot_ids = jnp.arange(experts * capacity, dtype=jnp.int32)
    slot_source = slot_ids // capacity
    slot_rank = slot_ids % capacity
    slot_live = slot_rank < arrived[slot_source]
    slot_pos = jnp.where(slot_live, offsets[slot_source] + slot_rank, slot_count)
    share_packed = lax.psum_scatter(
        hidden_part.astype(jnp.bfloat16), "head", scatter_dimension=1, tiled=True
    )
    share_width = share_packed.shape[1]
    padded_grad = jnp.concatenate(
        [share_packed, jnp.zeros((1, share_packed.shape[1]), jnp.bfloat16)], axis=0
    )
    returned = lax.all_to_all(
        padded_grad[slot_pos].reshape(experts, capacity, share_packed.shape[1]),
        "seq",
        split_axis=0,
        concat_axis=0,
        tiled=True,
    )
    share_grad = returned.reshape(experts * capacity, share_width)[slot_of]
    expert_grad = lax.all_gather(share_grad, "head", axis=1, tiled=True)
    grad_hidden = (full_rows.astype(jnp.float32) + expert_grad.astype(jnp.float32)).astype(
        jnp.bfloat16
    )
    head_grad = jnp.dot(grad_hidden, w_out.T, preferred_element_type=jnp.float32).astype(
        jnp.bfloat16
    )
    query_part = jnp.dot(queries.T, head_grad, preferred_element_type=jnp.float32)
    key_state, query_state = lax.psum(
        (jnp.dot(keys.T, values, preferred_element_type=jnp.float32), query_part), "seq"
    )
    key_round = key_state.astype(jnp.bfloat16)
    query_round = query_state.astype(jnp.bfloat16)
    grad_queries = (
        scaling * jnp.dot(head_grad, key_round.T, preferred_element_type=jnp.float32)
    ).astype(jnp.bfloat16)
    grad_keys = (
        scaling * jnp.dot(values, query_round.T, preferred_element_type=jnp.float32)
    ).astype(jnp.bfloat16)
    grad_values = (scaling * jnp.dot(keys, query_round, preferred_element_type=jnp.float32)).astype(
        jnp.bfloat16
    )
    return (grad_hidden, grad_queries, grad_keys, grad_values)


def solution(mesh):
    return jax.shard_map(
        step,
        mesh=mesh,
        in_specs=(
            P("seq", "head"),
            P("seq"),
            P(None, "seq"),
            P("seq", None, "head"),
            P("seq", "head", None),
            P("seq", "head"),
            P("seq", "head"),
            P("seq", "head"),
            P("seq", "head"),
            P("head", None),
        ),
        out_specs=(P("seq", None), P("seq", "head"), P("seq", "head"), P("seq", "head")),
        check_vma=False,
    )
```

```python
import functools
import math

import jax
import jax.numpy as jnp
from jax import lax
from jax.experimental import pallas as pl
from jax.experimental.pallas import tpu as pltpu
from jax.sharding import PartitionSpec as P

MESH = pl.DeviceIdType.MESH
F32 = jnp.float32
BF16 = jnp.bfloat16
ROWS = 16
VMEM_BYTES = 32 * 1024 * 1024


def iota(shape, dim):
    return lax.broadcasted_iota(jnp.int32, shape, dim)


def nn(a, b):
    return jnp.dot(a, b, preferred_element_type=F32)


def nt(a, b):
    return lax.dot_general(a, b, (((1,), (1,)), ((), ())), preferred_element_type=F32)


def kernel(
    n, pad, scaling,
    og_hbm, expert_hbm, counts_hbm, up_hbm, down_hbm, pre_hbm, q_hbm, k_hbm, v_hbm, wout_hbm,
    gh, gq, gk, gv,
    expert_of, counts, up, down, pre, wout, q, k, v, mask, grad_t, xsend, x, hsum,
    ysend, yrecv, rsend, ret, part, part_in, grads, wall, head_send, head_recv,
    ks_send, ks_recv, ks, qs_send, qs_recv, qs,
    load_sem, one_send, one_recv, disp_send, disp_recv, ax_send, ax_recv,
    hy_send, hy_recv, ret_send, ret_recv, st_send, st_recv, wall_send, wall_recv, head_ssem, head_rsem,
):
    s = lax.axis_index("seq")
    h = lax.axis_index("head")
    c = lax.rem(h, 2)
    y = lax.div(h, 2)
    sib = (s, h + 1 - 2 * c)
    far = (s, lax.rem(h + 2, 4))
    diag = (s, lax.rem(sib[1] + 2, 4))
    m = n // 2
    width, tok = og_hbm.shape
    pair = 2 * width
    rows = m * pad
    depth = x.shape[2]
    piece = ks.shape[1]
    mine = pl.ds(pl.multiple_of(y * pair, 128), pair)
    other = pl.ds(pl.multiple_of((1 - y) * pair, 128), pair)
    parity = lax.rem(s + c, 2)
    own_rows = pl.ds(pl.multiple_of(c * width, ROWS), width)
    sib_rows = pl.ds(pl.multiple_of((1 - c) * width, ROWS), width)

    def send(src, dst, ssem, rsem, to):
        return pltpu.make_async_remote_copy(
            src_ref=src, dst_ref=dst, send_sem=ssem, recv_sem=rsem, device_id=to, device_id_type=MESH
        )

    barrier = pltpu.get_barrier_semaphore()
    peers = [lax.rem(s + d, n) for d in range(1, n)]
    for p in peers:
        pl.semaphore_signal(barrier, inc=1, device_id=(p, h), device_id_type=MESH)
    for to in (sib, far, diag):
        pl.semaphore_signal(barrier, inc=1, device_id=to, device_id_type=MESH)
    loads = {}
    for i, (name, src, dst) in enumerate((
        ("expert", expert_hbm, expert_of), ("grad", og_hbm, grad_t.at[own_rows]),
        ("k", k_hbm, k), ("v", v_hbm, v), ("counts", counts_hbm, counts),
        ("pre", pre_hbm, pre.at[0]), ("down", down_hbm.at[0], down.at[0]),
        ("up", up_hbm.at[0], up.at[0]), ("wout", wout_hbm, wout),
        ("q", q_hbm, q),
    )):
        loads[name] = pltpu.make_async_copy(src, dst, load_sem.at[i])
        loads[name].start()

    pl.semaphore_wait(barrier, n + 2)
    pending = []

    def start(copy):
        copy.start()
        pending.append(copy)
        return copy

    loads["grad"].wait()
    spot = grad_t.at[own_rows]
    start(send(spot, spot, one_send.at[0], one_recv.at[0], sib))
    loads["expert"].wait()
    e_row = expert_of[...]
    eye = iota((tok, tok), 0) == iota((tok, tok), 1)
    e_col = jnp.sum(jnp.where(eye, e_row, 0), axis=1, keepdims=True)
    same = (e_col == e_row).astype(jnp.int32)
    below = iota((tok, tok), 0) < iota((tok, tok), 1)
    rank_row = jnp.sum(jnp.where(below, same, 0), axis=0, keepdims=True)
    live_row = lax.rem(e_row, 2) == parity
    slot_row = jnp.where(live_row, lax.div(e_row, 2) * pad + rank_row, -1)
    scatter = (iota((rows, tok), 0) == slot_row).astype(BF16)

    swaps = []
    for i, (name, both) in enumerate((("pre", pre), ("down", down), ("up", up))):
        loads[name].wait()
        swaps.append(start(send(both.at[0], both.at[1], one_send.at[3 + i], one_recv.at[3 + i], sib)))

    loads["wout"].wait()
    wall[h] = wout[:, mine]
    start(send(wout.at[:, other], wall.at[h], wall_send.at[0], wall_recv.at[0], far))
    start(send(wout.at[:, mine], wall.at[h], wall_send.at[1], wall_recv.at[1], sib))

    spot = grad_t.at[sib_rows]
    send(spot, spot, one_send.at[0], one_recv.at[0], sib).wait_recv()
    blocks = nt(scatter, grad_t[...]).astype(BF16)
    for i in range(m):
        xsend[i] = blocks[i * pad : (i + 1) * pad]
    turns = [*range(1, m), 0]
    order = [(j, lax.rem(s + c + 2 * j, n)) for j in turns]
    for j, p in order:
        copy = send(
            xsend.at[lax.div(p, 2)], x.at[lax.div(s, 2), :, mine],
            disp_send.at[j], disp_recv.at[lax.div(s, 2)], (p, h),
        )
        if j == 0:
            pl.when(c == 1)(copy.start)

            @pl.when(c == 0)
            def _():
                x[lax.div(s, 2), :, mine] = xsend[lax.div(s, 2)]
        else:
            start(copy)

    loads["counts"].wait()
    slot = iota((rows, 1), 0)
    source = 2 * lax.div(slot, pad) + parity
    before = iota((rows, n), 1) < source
    packed = jnp.sum(jnp.where(before, counts[...], 0), axis=1, keepdims=True) + lax.rem(slot, pad)
    unpack = (iota((rows, pre.shape[1]), 1) == packed).astype(BF16)
    mask[0] = nn(unpack, pre[0]).astype(BF16).reshape(m, pad, -1)

    near = [(j, lax.rem(s + c + 2 * j, n)) for j in sorted(range(m), key=lambda j: min(j, m - j))]
    for j, p in near:
        i = lax.div(p, 2)
        spot = x.at[i, :, mine]
        copy = send(spot, spot, disp_send.at[j], disp_recv.at[i], (p, h))
        if j == 0:
            pl.when(c == 1)(copy.wait_recv)
        else:
            copy.wait_recv()
        start(send(spot, spot, ax_send.at[j], ax_recv.at[j], far))

    spot = wall.at[far[1]]
    send(spot, spot, wall_send.at[0], wall_recv.at[0], far).wait_recv()
    start(send(spot, spot, wall_send.at[2], wall_recv.at[2], sib))

    loads["k"].wait()
    loads["v"].wait()
    ks_part = nn(k[...].T, v[...]).astype(BF16)
    for p in range(n):
        ks_send[p] = ks_part[p * piece : (p + 1) * piece]

    def state_scatter(at, source, dest):
        for d, p in enumerate(peers):
            start(send(source.at[p], dest.at[s], st_send.at[at, d], st_recv.at[at, s], (p, h)))
        dest[s] = source[s]

    def state_sum(at, dest, total):
        for p in peers:
            send(dest.at[p], dest.at[p], st_send.at[at, 0], st_recv.at[at, p], (p, h)).wait_recv()
        acc = dest[0].astype(F32)
        for p in range(1, n):
            acc = acc + dest[p].astype(F32)
        total[s] = acc.astype(BF16)
        for d, p in enumerate(peers):
            start(send(
                total.at[s], total.at[s], st_send.at[at + 1, d], st_recv.at[at + 1, s], (p, h)
            ))

    def state_wait(at, total):
        for p in peers:
            send(total.at[p], total.at[p], st_send.at[at, 0], st_recv.at[at, p], (p, h)).wait_recv()

    state_scatter(0, ks_send, ks_recv)

    swaps[0].wait_recv()
    mask[1] = nn(unpack, pre[1]).astype(BF16).reshape(m, pad, -1)
    swaps[1].wait_recv()
    swaps[2].wait_recv()
    group = max(m // 2, 1)
    mids = []
    for g in range(0, m, group):
        some = [(j, lax.div(p, 2)) for j, p in near[g : g + group]]
        ready = jnp.concatenate([x[i, :, mine] for _, i in some], axis=0)
        middle = [nt(ready, down[u, :, mine]) for u in range(2)]
        for j, i in some:
            spot = x.at[i, :, other]
            send(spot, spot, ax_send.at[j], ax_recv.at[j], far).wait_recv()
        ready = jnp.concatenate([x[i, :, other] for _, i in some], axis=0)
        mid = []
        for u in range(2):
            full_sum = middle[u] + nt(ready, down[u, :, other])
            live = jnp.concatenate([mask[u, i] for _, i in some], axis=0)
            mid.append(jnp.where(live > 0, full_sum, 0.0).astype(BF16))
        away = (nt(mid[0], up[0, other, :]) + nt(mid[1], up[1, other, :])).astype(BF16)
        for at, (j, i) in enumerate(some):
            ysend[i] = away[at * pad : (at + 1) * pad]
            start(send(ysend.at[i], yrecv.at[i], hy_send.at[j], hy_recv.at[j], far))
        mids.append((some, mid))
    for some, mid in mids:
        stay = nt(mid[0], up[0, mine, :]) + nt(mid[1], up[1, mine, :])
        for at, (j, i) in enumerate(some):
            hsum[i] = stay[at * pad : (at + 1) * pad]
    state_sum(0, ks_recv, ks)

    for j, p in near:
        i = lax.div(p, 2)
        spot = yrecv.at[i]
        send(spot, spot, hy_send.at[j], hy_recv.at[j], far).wait_recv()
        rsend[i] = (hsum[i] + yrecv[i].astype(F32)).astype(BF16)
        copy = send(
            rsend.at[i], ret.at[lax.div(s, 2)], ret_send.at[j], ret_recv.at[lax.div(s, 2)], (p, h)
        )
        if j == 0:
            pl.when(c == 1)(copy.start)

            @pl.when(c == 0)
            def _():
                ret[lax.div(s, 2)] = rsend[lax.div(s, 2)]
        else:
            start(copy)
    above = iota((tok, tok), 1) < iota((tok, tok), 0)
    rank_col = jnp.sum(jnp.where(above, same, 0), axis=1, keepdims=True)
    live_col = lax.rem(e_col, 2) == parity
    slot_col = jnp.where(live_col, lax.div(e_col, 2) * pad + rank_col, -1)
    combine = (iota((tok, rows), 1) == slot_col).astype(BF16)
    own = jnp.where(live_col, grad_t[...].astype(F32).T, 0.0)
    loads["q"].wait()
    q_t = q[...].T
    spot = wall.at[sib[1]]
    send(spot, spot, wall_send.at[1], wall_recv.at[1], sib).wait_recv()
    spot = wall.at[diag[1]]
    send(spot, spot, wall_send.at[2], wall_recv.at[2], sib).wait_recv()
    state_wait(1, ks)
    for j, p in near:
        i = lax.div(p, 2)
        copy = send(ret.at[i], ret.at[i], ret_send.at[j], ret_recv.at[i], (p, h))
        if j == 0:
            pl.when(c == 1)(copy.wait_recv)
        else:
            copy.wait_recv()
    half = (own + nn(combine, ret[...].reshape(rows, pair))).astype(BF16)
    dim = n * piece
    cut = dim // 2
    for b in range(2):
        for i, to in enumerate((diag, far, sib)):
            head_send[b, i] = nt(half, wall[to[1], b * cut : (b + 1) * cut, :]).astype(BF16)
            start(send(
                head_send.at[b, i], head_recv.at[b, i], head_ssem.at[b, i], head_rsem.at[b, i], to
            ))
    part[...] = half
    start(send(part, part_in, one_send.at[1], one_recv.at[1], sib))
    head_grad = []
    for b in range(2):
        head_sum = nt(half, wall[h, b * cut : (b + 1) * cut, :])
        for i, to in ((2, sib), (1, far), (0, diag)):
            spot = head_recv.at[b, i]
            send(spot, spot, head_ssem.at[b, i], head_rsem.at[b, i], to).wait_recv()
            head_sum = head_sum + head_recv[b, i].astype(F32)
        head_grad.append(head_sum.astype(BF16))
        qs_part = nn(q_t, head_grad[b]).astype(BF16)
        for p in range(n):
            qs_send[b, p] = qs_part[p * piece : (p + 1) * piece]
        state_scatter(2 + 2 * b, qs_send.at[b], qs_recv.at[b])
    send(part, part_in, one_send.at[1], one_recv.at[1], sib).wait_recv()
    grads[:, mine] = part[...] + part_in[...]
    spot = grads.at[:, mine]
    start(send(spot, spot, one_send.at[2], one_recv.at[2], far))
    k_round = ks[...].reshape(dim, dim)
    gq[...] = (
        scaling * (nt(head_grad[0], k_round[:, :cut]) + nt(head_grad[1], k_round[:, cut:]))
    ).astype(BF16)
    for b in range(2):
        state_sum(2 + 2 * b, qs_recv.at[b], qs.at[b])
    spot = grads.at[:, other]
    send(spot, spot, one_send.at[2], one_recv.at[2], far).wait_recv()
    gh[...] = grads[...]
    key_sum = 0.0
    for b in range(2):
        state_wait(3 + 2 * b, qs.at[b])
        q_round = qs[b].reshape(dim, cut)
        gv[:, b * cut : (b + 1) * cut] = (scaling * nn(k[...], q_round)).astype(BF16)
        key_sum = key_sum + nt(v[:, b * cut : (b + 1) * cut], q_round)
    gk[...] = (scaling * key_sum).astype(BF16)

    for copy in pending:
        copy.wait_send()

    @pl.when(c == 1)
    def _():
        send(xsend.at[0], xsend.at[0], disp_send.at[0], disp_recv.at[0], sib).wait_send()
        send(rsend.at[0], rsend.at[0], ret_send.at[0], ret_recv.at[0], sib).wait_send()


def write_out(*refs):
    count = len(refs) // 2
    sem = refs[-1]
    copies = [pltpu.make_async_copy(refs[i], refs[count + i], sem.at[i]) for i in range(count)]
    for copy in copies:
        copy.start()
    for copy in copies:
        copy.wait()


def fused(out_grad, expert_of, counts, w_up, w_down, pre_act, queries, keys, values, w_out):
    n = lax.axis_size("seq")
    m = n // 2
    tok, width = out_grad.shape
    slots = pre_act.shape[0]
    cap = slots // n
    pad = -(-cap // ROWS) * ROWS
    rows = m * pad
    depth, hidden = w_up.shape[1:]
    dim = queries.shape[1]
    pair = 2 * width
    piece = dim // n
    scaling = 1.0 / math.sqrt(dim * tok * n)
    hbm = pl.BlockSpec(memory_space=pltpu.HBM)
    vmem = pl.BlockSpec(memory_space=pltpu.VMEM)
    dma = pltpu.SemaphoreType.DMA

    def buf(*shape, dtype=BF16):
        return pltpu.VMEM(shape, dtype)

    state = buf(n, piece, dim)
    halves = buf(2, n, piece, dim // 2)
    out = jax.ShapeDtypeStruct((tok, dim), BF16)
    outs = (jax.ShapeDtypeStruct((tok, depth), BF16), out, out, out)
    results = pl.pallas_call(
        functools.partial(kernel, n, pad, scaling),
        out_shape=outs,
        in_specs=[hbm] * 10,
        out_specs=(vmem,) * 4,
        scratch_shapes=[
            buf(1, tok, dtype=jnp.int32), buf(1, n, dtype=jnp.int32),
            buf(2, depth, hidden), buf(2, hidden, depth), buf(2, slots, hidden), buf(dim, depth),
            buf(tok, dim), buf(tok, dim), buf(tok, dim), buf(2, m, pad, hidden),
            buf(pair, tok), buf(m, pad, pair), buf(m, pad, depth), buf(m, pad, pair, dtype=F32),
            buf(m, pad, pair), buf(m, pad, pair), buf(m, pad, pair), buf(m, pad, pair),
            buf(tok, pair), buf(tok, pair), buf(tok, depth),
            buf(4, dim, pair), buf(2, 3, tok, dim // 2), buf(2, 3, tok, dim // 2),
            state, state, state, halves, halves, halves,
            dma((10,)), dma((6,)), dma((6,)), dma((m,)), dma((m,)), dma((m,)), dma((m,)),
            dma((m,)), dma((m,)), dma((m,)), dma((m,)), dma((6, n)), dma((6, n)), dma((3,)), dma((3,)),
            dma((2, 3)), dma((2, 3)),
        ],
        compiler_params=pltpu.CompilerParams(
            collective_id=0, has_side_effects=True, vmem_limit_bytes=VMEM_BYTES
        ),
    )(*(pltpu.with_memory_space_constraint(operand, pltpu.HBM) for operand in (
        out_grad.T, expert_of.reshape(1, tok), counts.T, w_up, w_down, pre_act,
        queries, keys, values, w_out,
    )))
    return pl.pallas_call(
        write_out,
        out_shape=outs,
        in_specs=[vmem] * 4,
        out_specs=(hbm,) * 4,
        scratch_shapes=[dma((4,))],
        compiler_params=pltpu.CompilerParams(vmem_limit_bytes=VMEM_BYTES // 8),
    )(*results)


def step(*arrays):
    n, heads = lax.axis_size("seq"), lax.axis_size("head")
    width, dim = arrays[0].shape[1], arrays[6].shape[1]
    fits = heads == 4 and n % 2 == 0 and dim % (n * ROWS) == 0 and dim % 256 == 0 and 2 * width % 128 == 0
    return (fused if fits else shards)(*arrays)


def shards(out_grad, expert_of, counts, w_up, w_down, pre_act, queries, keys, values, w_out):
    experts = lax.axis_size("seq")
    tok_rows = out_grad.shape[0]
    slot_count = pre_act.shape[0]
    capacity = slot_count // experts
    head_dim = queries.shape[1]
    scaling = 1.0 / math.sqrt(head_dim * tok_rows * experts)
    full_rows = lax.all_gather(out_grad, "head", axis=1, tiled=True)
    expert_ids = jnp.arange(experts, dtype=jnp.int32)
    onehot = (expert_of[:, None] == expert_ids[None, :]).astype(jnp.int32)
    token_rank = jnp.sum((jnp.cumsum(onehot, axis=0) - 1) * onehot, axis=1)
    slot_of = expert_of * capacity + token_rank
    token_of_slot = (
        jnp.full((experts * capacity,), tok_rows, jnp.int32)
        .at[slot_of]
        .set(jnp.arange(tok_rows, dtype=jnp.int32))
    )
    arrived = counts[:, 0]
    offsets = jnp.cumsum(arrived) - arrived
    arrived_total = jnp.sum(arrived)
    packed_ids = jnp.arange(slot_count, dtype=jnp.int32)
    source = jnp.sum((offsets[None, :] <= packed_ids[:, None]).astype(jnp.int32), axis=1) - 1
    within = packed_ids - offsets[source]
    packed_live = packed_ids < arrived_total
    flat_pos = jnp.where(packed_live, source * capacity + within, experts * capacity)
    down_local = w_down[0]
    up_local = w_up[0]
    padded = jnp.concatenate(
        [full_rows, jnp.zeros((1, full_rows.shape[1]), full_rows.dtype)], axis=0
    )
    received = lax.all_to_all(
        padded[token_of_slot].reshape(experts, capacity, full_rows.shape[1]),
        "seq",
        split_axis=0,
        concat_axis=0,
        tiled=True,
    )
    flat_rows = received.reshape(experts * capacity, received.shape[2])
    padded = jnp.concatenate(
        [flat_rows, jnp.zeros((1, flat_rows.shape[1]), flat_rows.dtype)], axis=0
    )
    middle = jnp.dot(padded[flat_pos], down_local.T, preferred_element_type=jnp.float32)
    mid_grad = jnp.where(pre_act > 0, middle, jnp.zeros_like(middle)).astype(jnp.bfloat16)
    hidden_part = jnp.dot(mid_grad, up_local.T, preferred_element_type=jnp.float32)
    slot_ids = jnp.arange(experts * capacity, dtype=jnp.int32)
    slot_source = slot_ids // capacity
    slot_rank = slot_ids % capacity
    slot_live = slot_rank < arrived[slot_source]
    slot_pos = jnp.where(slot_live, offsets[slot_source] + slot_rank, slot_count)
    share_packed = lax.psum_scatter(
        hidden_part.astype(jnp.bfloat16), "head", scatter_dimension=1, tiled=True
    )
    share_width = share_packed.shape[1]
    padded_grad = jnp.concatenate(
        [share_packed, jnp.zeros((1, share_packed.shape[1]), jnp.bfloat16)], axis=0
    )
    returned = lax.all_to_all(
        padded_grad[slot_pos].reshape(experts, capacity, share_packed.shape[1]),
        "seq",
        split_axis=0,
        concat_axis=0,
        tiled=True,
    )
    share_grad = returned.reshape(experts * capacity, share_width)[slot_of]
    expert_grad = lax.all_gather(share_grad, "head", axis=1, tiled=True)
    grad_hidden = (full_rows.astype(jnp.float32) + expert_grad.astype(jnp.float32)).astype(
        jnp.bfloat16
    )
    head_grad = jnp.dot(grad_hidden, w_out.T, preferred_element_type=jnp.float32).astype(
        jnp.bfloat16
    )
    query_part = jnp.dot(queries.T, head_grad, preferred_element_type=jnp.float32)
    key_state, query_state = lax.psum(
        (jnp.dot(keys.T, values, preferred_element_type=jnp.float32), query_part), "seq"
    )
    key_round = key_state.astype(jnp.bfloat16)
    query_round = query_state.astype(jnp.bfloat16)
    grad_queries = (
        scaling * jnp.dot(head_grad, key_round.T, preferred_element_type=jnp.float32)
    ).astype(jnp.bfloat16)
    grad_keys = (
        scaling * jnp.dot(values, query_round.T, preferred_element_type=jnp.float32)
    ).astype(jnp.bfloat16)
    grad_values = (scaling * jnp.dot(keys, query_round, preferred_element_type=jnp.float32)).astype(
        jnp.bfloat16
    )
    return (grad_hidden, grad_queries, grad_keys, grad_values)


def solution(mesh):
    return jax.shard_map(
        step,
        mesh=mesh,
        in_specs=(
            P("seq", "head"),
            P("seq"),
            P(None, "seq"),
            P("seq", None, "head"),
            P("seq", "head", None),
            P("seq", "head"),
            P("seq", "head"),
            P("seq", "head"),
            P("seq", "head"),
            P("head", None),
        ),
        out_specs=(P("seq", None), P("seq", "head"), P("seq", "head"), P("seq", "head")),
        check_vma=False,
    )
```

```python
import functools
import math

import jax
import jax.numpy as jnp
from jax import lax
from jax.experimental import pallas as pl
from jax.experimental.pallas import tpu as pltpu
from jax.sharding import PartitionSpec as P

MESH = pl.DeviceIdType.MESH
F32 = jnp.float32
BF16 = jnp.bfloat16
ROWS = 16
VMEM_BYTES = 32 * 1024 * 1024


def iota(shape, dim):
    return lax.broadcasted_iota(jnp.int32, shape, dim)


def nn(a, b):
    return jnp.dot(a, b, preferred_element_type=F32)


def nt(a, b):
    return lax.dot_general(a, b, (((1,), (1,)), ((), ())), preferred_element_type=F32)


def kernel(
    n, pad, scaling,
    og_hbm, expert_hbm, counts_hbm, up_hbm, down_hbm, pre_hbm, q_hbm, k_hbm, v_hbm, wout_hbm,
    gh, gq, gk, gv,
    expert_of, counts, up, down, pre, wout, q, k, v, mask, grad_t, xsend, x, hsum,
    ysend, yrecv, rsend, ret, part, part_in, grads, wall, head_send, head_recv,
    ks_send, ks_recv, ks, qs_send, qs_recv, qs,
    load_sem, one_send, one_recv, disp_send, disp_recv, ax_send, ax_recv,
    hy_send, hy_recv, ret_send, ret_recv, st_send, st_recv, wall_send, wall_recv, head_ssem, head_rsem,
):
    s = lax.axis_index("seq")
    h = lax.axis_index("head")
    c = lax.rem(h, 2)
    y = lax.div(h, 2)
    sib = (s, h + 1 - 2 * c)
    far = (s, lax.rem(h + 2, 4))
    diag = (s, lax.rem(sib[1] + 2, 4))
    m = n // 2
    width, tok = og_hbm.shape
    pair = 2 * width
    rows = m * pad
    depth = x.shape[2]
    piece = ks.shape[1]
    mine = pl.ds(pl.multiple_of(y * pair, 128), pair)
    other = pl.ds(pl.multiple_of((1 - y) * pair, 128), pair)
    parity = lax.rem(s + c, 2)
    own_rows = pl.ds(pl.multiple_of(c * width, ROWS), width)
    sib_rows = pl.ds(pl.multiple_of((1 - c) * width, ROWS), width)

    def send(src, dst, ssem, rsem, to):
        return pltpu.make_async_remote_copy(
            src_ref=src, dst_ref=dst, send_sem=ssem, recv_sem=rsem, device_id=to, device_id_type=MESH
        )

    barrier = pltpu.get_barrier_semaphore()
    peers = [lax.rem(s + d, n) for d in range(1, n)]
    for p in peers:
        pl.semaphore_signal(barrier, inc=1, device_id=(p, h), device_id_type=MESH)
    for to in (sib, far, diag):
        pl.semaphore_signal(barrier, inc=1, device_id=to, device_id_type=MESH)
    loads = {}
    for i, (name, src, dst) in enumerate((
        ("expert", expert_hbm, expert_of), ("grad", og_hbm, grad_t.at[own_rows]),
        ("wout", wout_hbm, wout), ("k", k_hbm, k), ("v", v_hbm, v), ("counts", counts_hbm, counts),
        ("pre", pre_hbm, pre.at[0]), ("down", down_hbm.at[0], down.at[0]),
        ("up", up_hbm.at[0], up.at[0]),
        ("q", q_hbm, q),
    )):
        loads[name] = pltpu.make_async_copy(src, dst, load_sem.at[i])
        loads[name].start()

    pl.semaphore_wait(barrier, n + 2)
    pending = []

    def start(copy):
        copy.start()
        pending.append(copy)
        return copy

    loads["grad"].wait()
    spot = grad_t.at[own_rows]
    start(send(spot, spot, one_send.at[0], one_recv.at[0], sib))
    cut = n * piece // 2

    def wall_rows(k):
        return pl.ds(k * cut, cut)

    def wall_swap(k):
        start(send(
            wout.at[wall_rows(k), other], wall.at[h, wall_rows(k)],
            wall_send.at[k], wall_recv.at[k], far,
        ))

    def wall_relay(k):
        spot = wall.at[far[1], wall_rows(k)]
        send(spot, spot, wall_send.at[k], wall_recv.at[k], far).wait_recv()
        start(send(spot, spot, wall_send.at[3 + k], wall_recv.at[3 + k], sib))

    loads["wout"].wait()
    wall_swap(0)

    loads["expert"].wait()
    e_row = expert_of[...]
    eye = iota((tok, tok), 0) == iota((tok, tok), 1)
    e_col = jnp.sum(jnp.where(eye, e_row, 0), axis=1, keepdims=True)
    same = (e_col == e_row).astype(jnp.int32)
    below = iota((tok, tok), 0) < iota((tok, tok), 1)
    rank_row = jnp.sum(jnp.where(below, same, 0), axis=0, keepdims=True)
    live_row = lax.rem(e_row, 2) == parity
    slot_row = jnp.where(live_row, lax.div(e_row, 2) * pad + rank_row, -1)
    scatter = (iota((rows, tok), 0) == slot_row).astype(BF16)

    swaps = []
    for i, (name, both) in enumerate((("pre", pre), ("down", down), ("up", up))):
        loads[name].wait()
        swaps.append(start(send(both.at[0], both.at[1], one_send.at[3 + i], one_recv.at[3 + i], sib)))

    wall[h] = wout[:, mine]
    start(send(wout.at[:, mine], wall.at[h], wall_send.at[2], wall_recv.at[2], sib))

    spot = grad_t.at[sib_rows]
    send(spot, spot, one_send.at[0], one_recv.at[0], sib).wait_recv()
    blocks = nt(scatter, grad_t[...]).astype(BF16)
    for i in range(m):
        xsend[i] = blocks[i * pad : (i + 1) * pad]
    turns = [*range(1, m), 0]
    order = [(j, lax.rem(s + c + 2 * j, n)) for j in turns]
    for j, p in order:
        copy = send(
            xsend.at[lax.div(p, 2)], x.at[lax.div(s, 2), :, mine],
            disp_send.at[j], disp_recv.at[lax.div(s, 2)], (p, h),
        )
        if j == 0:
            pl.when(c == 1)(copy.start)

            @pl.when(c == 0)
            def _():
                x[lax.div(s, 2), :, mine] = xsend[lax.div(s, 2)]
        else:
            start(copy)

    loads["counts"].wait()
    slot = iota((rows, 1), 0)
    source = 2 * lax.div(slot, pad) + parity
    before = iota((rows, n), 1) < source
    packed = jnp.sum(jnp.where(before, counts[...], 0), axis=1, keepdims=True) + lax.rem(slot, pad)
    unpack = (iota((rows, pre.shape[1]), 1) == packed).astype(BF16)
    mask[0] = nn(unpack, pre[0]).astype(BF16).reshape(m, pad, -1)

    near = [(j, lax.rem(s + c + 2 * j, n)) for j in sorted(range(m), key=lambda j: min(j, m - j))]
    for j, p in near:
        i = lax.div(p, 2)
        spot = x.at[i, :, mine]
        copy = send(spot, spot, disp_send.at[j], disp_recv.at[i], (p, h))
        if j == 0:
            pl.when(c == 1)(copy.wait_recv)
        else:
            copy.wait_recv()
        start(send(spot, spot, ax_send.at[j], ax_recv.at[j], far))

    wall_relay(0)

    loads["k"].wait()
    loads["v"].wait()
    ks_part = nn(k[...].T, v[...]).astype(BF16)
    for p in range(n):
        ks_send[p] = ks_part[p * piece : (p + 1) * piece]

    def state_scatter(at, source, dest):
        for d, p in enumerate(peers):
            start(send(source.at[p], dest.at[s], st_send.at[at, d], st_recv.at[at, s], (p, h)))
        dest[s] = source[s]

    def state_sum(at, dest, total):
        for p in peers:
            send(dest.at[p], dest.at[p], st_send.at[at, 0], st_recv.at[at, p], (p, h)).wait_recv()
        acc = dest[0].astype(F32)
        for p in range(1, n):
            acc = acc + dest[p].astype(F32)
        total[s] = acc.astype(BF16)
        for d, p in enumerate(peers):
            start(send(
                total.at[s], total.at[s], st_send.at[at + 1, d], st_recv.at[at + 1, s], (p, h)
            ))

    def state_wait(at, total):
        for p in peers:
            send(total.at[p], total.at[p], st_send.at[at, 0], st_recv.at[at, p], (p, h)).wait_recv()

    state_scatter(0, ks_send, ks_recv)

    group = max(m // 2, 1)
    groups = [
        [(j, lax.div(p, 2)) for j, p in near[g : g + group]] for g in range(0, m, group)
    ]
    firsts = [jnp.concatenate([x[i, :, mine] for _, i in some], axis=0) for some in groups]
    middles = [[nt(ready, down[0, :, mine])] for ready in firsts]
    swaps[0].wait_recv()
    mask[1] = nn(unpack, pre[1]).astype(BF16).reshape(m, pad, -1)
    swaps[1].wait_recv()
    for middle, ready in zip(middles, firsts):
        middle.append(nt(ready, down[1, :, mine]))
    swaps[2].wait_recv()
    mids = []
    for some, middle in zip(groups, middles):
        for j, i in some:
            spot = x.at[i, :, other]
            send(spot, spot, ax_send.at[j], ax_recv.at[j], far).wait_recv()
        ready = jnp.concatenate([x[i, :, other] for _, i in some], axis=0)
        mid = []
        for u in range(2):
            full_sum = middle[u] + nt(ready, down[u, :, other])
            live = jnp.concatenate([mask[u, i] for _, i in some], axis=0)
            mid.append(jnp.where(live > 0, full_sum, 0.0).astype(BF16))
        away = (nt(mid[0], up[0, other, :]) + nt(mid[1], up[1, other, :])).astype(BF16)
        for at, (j, i) in enumerate(some):
            ysend[i] = away[at * pad : (at + 1) * pad]
            start(send(ysend.at[i], yrecv.at[i], hy_send.at[j], hy_recv.at[j], far))
        mids.append((some, mid))
    wall_swap(1)
    for some, mid in mids:
        stay = nt(mid[0], up[0, mine, :]) + nt(mid[1], up[1, mine, :])
        for at, (j, i) in enumerate(some):
            hsum[i] = stay[at * pad : (at + 1) * pad]
    state_sum(0, ks_recv, ks)

    for j, p in near:
        i = lax.div(p, 2)
        spot = yrecv.at[i]
        send(spot, spot, hy_send.at[j], hy_recv.at[j], far).wait_recv()
        rsend[i] = (hsum[i] + yrecv[i].astype(F32)).astype(BF16)
        copy = send(
            rsend.at[i], ret.at[lax.div(s, 2)], ret_send.at[j], ret_recv.at[lax.div(s, 2)], (p, h)
        )
        if j == 0:
            pl.when(c == 1)(copy.start)

            @pl.when(c == 0)
            def _():
                ret[lax.div(s, 2)] = rsend[lax.div(s, 2)]
        else:
            start(copy)
    above = iota((tok, tok), 1) < iota((tok, tok), 0)
    rank_col = jnp.sum(jnp.where(above, same, 0), axis=1, keepdims=True)
    live_col = lax.rem(e_col, 2) == parity
    slot_col = jnp.where(live_col, lax.div(e_col, 2) * pad + rank_col, -1)
    combine = (iota((tok, rows), 1) == slot_col).astype(BF16)
    own = jnp.where(live_col, grad_t[...].astype(F32).T, 0.0)
    loads["q"].wait()
    q_t = q[...].T
    wall_relay(1)
    spot = wall.at[sib[1]]
    send(spot, spot, wall_send.at[2], wall_recv.at[2], sib).wait_recv()
    for b in range(2):
        spot = wall.at[diag[1], wall_rows(b)]
        send(spot, spot, wall_send.at[3 + b], wall_recv.at[3 + b], sib).wait_recv()
    state_wait(1, ks)
    for j, p in near:
        i = lax.div(p, 2)
        copy = send(ret.at[i], ret.at[i], ret_send.at[j], ret_recv.at[i], (p, h))
        if j == 0:
            pl.when(c == 1)(copy.wait_recv)
        else:
            copy.wait_recv()
    half = (own + nn(combine, ret[...].reshape(rows, pair))).astype(BF16)
    dim = n * piece
    for b in range(2):
        for i, to in enumerate((diag, far, sib)):
            head_send[b, i] = nt(half, wall[to[1], b * cut : (b + 1) * cut, :]).astype(BF16)
            start(send(
                head_send.at[b, i], head_recv.at[b, i], head_ssem.at[b, i], head_rsem.at[b, i], to
            ))
    part[...] = half
    start(send(part, part_in, one_send.at[1], one_recv.at[1], sib))
    head_grad = []
    for b in range(2):
        head_sum = nt(half, wall[h, b * cut : (b + 1) * cut, :])
        for i, to in ((2, sib), (1, far), (0, diag)):
            spot = head_recv.at[b, i]
            send(spot, spot, head_ssem.at[b, i], head_rsem.at[b, i], to).wait_recv()
            head_sum = head_sum + head_recv[b, i].astype(F32)
        head_grad.append(head_sum.astype(BF16))
        qs_part = nn(q_t, head_grad[b]).astype(BF16)
        for p in range(n):
            qs_send[b, p] = qs_part[p * piece : (p + 1) * piece]
        state_scatter(2 + 2 * b, qs_send.at[b], qs_recv.at[b])
    send(part, part_in, one_send.at[1], one_recv.at[1], sib).wait_recv()
    grads[:, mine] = part[...] + part_in[...]
    spot = grads.at[:, mine]
    start(send(spot, spot, one_send.at[2], one_recv.at[2], far))
    k_round = ks[...].reshape(dim, dim)
    gq[...] = (
        scaling * (nt(head_grad[0], k_round[:, :cut]) + nt(head_grad[1], k_round[:, cut:]))
    ).astype(BF16)
    for b in range(2):
        state_sum(2 + 2 * b, qs_recv.at[b], qs.at[b])
    spot = grads.at[:, other]
    send(spot, spot, one_send.at[2], one_recv.at[2], far).wait_recv()
    gh[...] = grads[...]
    key_sum = 0.0
    for b in range(2):
        state_wait(3 + 2 * b, qs.at[b])
        q_round = qs[b].reshape(dim, cut)
        gv[:, b * cut : (b + 1) * cut] = (scaling * nn(k[...], q_round)).astype(BF16)
        key_sum = key_sum + nt(v[:, b * cut : (b + 1) * cut], q_round)
    gk[...] = (scaling * key_sum).astype(BF16)

    for copy in pending:
        copy.wait_send()

    @pl.when(c == 1)
    def _():
        send(xsend.at[0], xsend.at[0], disp_send.at[0], disp_recv.at[0], sib).wait_send()
        send(rsend.at[0], rsend.at[0], ret_send.at[0], ret_recv.at[0], sib).wait_send()


def write_out(*refs):
    count = len(refs) // 2
    sem = refs[-1]
    copies = [pltpu.make_async_copy(refs[i], refs[count + i], sem.at[i]) for i in range(count)]
    for copy in copies:
        copy.start()
    for copy in copies:
        copy.wait()


def fused(out_grad, expert_of, counts, w_up, w_down, pre_act, queries, keys, values, w_out):
    n = lax.axis_size("seq")
    m = n // 2
    tok, width = out_grad.shape
    slots = pre_act.shape[0]
    cap = slots // n
    pad = -(-cap // ROWS) * ROWS
    rows = m * pad
    depth, hidden = w_up.shape[1:]
    dim = queries.shape[1]
    pair = 2 * width
    piece = dim // n
    scaling = 1.0 / math.sqrt(dim * tok * n)
    hbm = pl.BlockSpec(memory_space=pltpu.HBM)
    vmem = pl.BlockSpec(memory_space=pltpu.VMEM)
    dma = pltpu.SemaphoreType.DMA

    def buf(*shape, dtype=BF16):
        return pltpu.VMEM(shape, dtype)

    state = buf(n, piece, dim)
    halves = buf(2, n, piece, dim // 2)
    out = jax.ShapeDtypeStruct((tok, dim), BF16)
    outs = (jax.ShapeDtypeStruct((tok, depth), BF16), out, out, out)
    results = pl.pallas_call(
        functools.partial(kernel, n, pad, scaling),
        out_shape=outs,
        in_specs=[hbm] * 10,
        out_specs=(vmem,) * 4,
        scratch_shapes=[
            buf(1, tok, dtype=jnp.int32), buf(1, n, dtype=jnp.int32),
            buf(2, depth, hidden), buf(2, hidden, depth), buf(2, slots, hidden), buf(dim, depth),
            buf(tok, dim), buf(tok, dim), buf(tok, dim), buf(2, m, pad, hidden),
            buf(pair, tok), buf(m, pad, pair), buf(m, pad, depth), buf(m, pad, pair, dtype=F32),
            buf(m, pad, pair), buf(m, pad, pair), buf(m, pad, pair), buf(m, pad, pair),
            buf(tok, pair), buf(tok, pair), buf(tok, depth),
            buf(4, dim, pair), buf(2, 3, tok, dim // 2), buf(2, 3, tok, dim // 2),
            state, state, state, halves, halves, halves,
            dma((10,)), dma((6,)), dma((6,)), dma((m,)), dma((m,)), dma((m,)), dma((m,)),
            dma((m,)), dma((m,)), dma((m,)), dma((m,)), dma((6, n)), dma((6, n)), dma((5,)), dma((5,)),
            dma((2, 3)), dma((2, 3)),
        ],
        compiler_params=pltpu.CompilerParams(
            collective_id=0, has_side_effects=True, vmem_limit_bytes=VMEM_BYTES
        ),
    )(*(pltpu.with_memory_space_constraint(operand, pltpu.HBM) for operand in (
        out_grad.T, expert_of.reshape(1, tok), counts.T, w_up, w_down, pre_act,
        queries, keys, values, w_out,
    )))
    return pl.pallas_call(
        write_out,
        out_shape=outs,
        in_specs=[vmem] * 4,
        out_specs=(hbm,) * 4,
        scratch_shapes=[dma((4,))],
        compiler_params=pltpu.CompilerParams(vmem_limit_bytes=VMEM_BYTES // 8),
    )(*results)


def step(*arrays):
    n, heads = lax.axis_size("seq"), lax.axis_size("head")
    width, dim = arrays[0].shape[1], arrays[6].shape[1]
    fits = heads == 4 and n % 2 == 0 and dim % (n * ROWS) == 0 and dim % 256 == 0 and 2 * width % 128 == 0
    return (fused if fits else shards)(*arrays)


def shards(out_grad, expert_of, counts, w_up, w_down, pre_act, queries, keys, values, w_out):
    experts = lax.axis_size("seq")
    tok_rows = out_grad.shape[0]
    slot_count = pre_act.shape[0]
    capacity = slot_count // experts
    head_dim = queries.shape[1]
    scaling = 1.0 / math.sqrt(head_dim * tok_rows * experts)
    full_rows = lax.all_gather(out_grad, "head", axis=1, tiled=True)
    expert_ids = jnp.arange(experts, dtype=jnp.int32)
    onehot = (expert_of[:, None] == expert_ids[None, :]).astype(jnp.int32)
    token_rank = jnp.sum((jnp.cumsum(onehot, axis=0) - 1) * onehot, axis=1)
    slot_of = expert_of * capacity + token_rank
    token_of_slot = (
        jnp.full((experts * capacity,), tok_rows, jnp.int32)
        .at[slot_of]
        .set(jnp.arange(tok_rows, dtype=jnp.int32))
    )
    arrived = counts[:, 0]
    offsets = jnp.cumsum(arrived) - arrived
    arrived_total = jnp.sum(arrived)
    packed_ids = jnp.arange(slot_count, dtype=jnp.int32)
    source = jnp.sum((offsets[None, :] <= packed_ids[:, None]).astype(jnp.int32), axis=1) - 1
    within = packed_ids - offsets[source]
    packed_live = packed_ids < arrived_total
    flat_pos = jnp.where(packed_live, source * capacity + within, experts * capacity)
    down_local = w_down[0]
    up_local = w_up[0]
    padded = jnp.concatenate(
        [full_rows, jnp.zeros((1, full_rows.shape[1]), full_rows.dtype)], axis=0
    )
    received = lax.all_to_all(
        padded[token_of_slot].reshape(experts, capacity, full_rows.shape[1]),
        "seq",
        split_axis=0,
        concat_axis=0,
        tiled=True,
    )
    flat_rows = received.reshape(experts * capacity, received.shape[2])
    padded = jnp.concatenate(
        [flat_rows, jnp.zeros((1, flat_rows.shape[1]), flat_rows.dtype)], axis=0
    )
    middle = jnp.dot(padded[flat_pos], down_local.T, preferred_element_type=jnp.float32)
    mid_grad = jnp.where(pre_act > 0, middle, jnp.zeros_like(middle)).astype(jnp.bfloat16)
    hidden_part = jnp.dot(mid_grad, up_local.T, preferred_element_type=jnp.float32)
    slot_ids = jnp.arange(experts * capacity, dtype=jnp.int32)
    slot_source = slot_ids // capacity
    slot_rank = slot_ids % capacity
    slot_live = slot_rank < arrived[slot_source]
    slot_pos = jnp.where(slot_live, offsets[slot_source] + slot_rank, slot_count)
    share_packed = lax.psum_scatter(
        hidden_part.astype(jnp.bfloat16), "head", scatter_dimension=1, tiled=True
    )
    share_width = share_packed.shape[1]
    padded_grad = jnp.concatenate(
        [share_packed, jnp.zeros((1, share_packed.shape[1]), jnp.bfloat16)], axis=0
    )
    returned = lax.all_to_all(
        padded_grad[slot_pos].reshape(experts, capacity, share_packed.shape[1]),
        "seq",
        split_axis=0,
        concat_axis=0,
        tiled=True,
    )
    share_grad = returned.reshape(experts * capacity, share_width)[slot_of]
    expert_grad = lax.all_gather(share_grad, "head", axis=1, tiled=True)
    grad_hidden = (full_rows.astype(jnp.float32) + expert_grad.astype(jnp.float32)).astype(
        jnp.bfloat16
    )
    head_grad = jnp.dot(grad_hidden, w_out.T, preferred_element_type=jnp.float32).astype(
        jnp.bfloat16
    )
    query_part = jnp.dot(queries.T, head_grad, preferred_element_type=jnp.float32)
    key_state, query_state = lax.psum(
        (jnp.dot(keys.T, values, preferred_element_type=jnp.float32), query_part), "seq"
    )
    key_round = key_state.astype(jnp.bfloat16)
    query_round = query_state.astype(jnp.bfloat16)
    grad_queries = (
        scaling * jnp.dot(head_grad, key_round.T, preferred_element_type=jnp.float32)
    ).astype(jnp.bfloat16)
    grad_keys = (
        scaling * jnp.dot(values, query_round.T, preferred_element_type=jnp.float32)
    ).astype(jnp.bfloat16)
    grad_values = (scaling * jnp.dot(keys, query_round, preferred_element_type=jnp.float32)).astype(
        jnp.bfloat16
    )
    return (grad_hidden, grad_queries, grad_keys, grad_values)


def solution(mesh):
    return jax.shard_map(
        step,
        mesh=mesh,
        in_specs=(
            P("seq", "head"),
            P("seq"),
            P(None, "seq"),
            P("seq", None, "head"),
            P("seq", "head", None),
            P("seq", "head"),
            P("seq", "head"),
            P("seq", "head"),
            P("seq", "head"),
            P("head", None),
        ),
        out_specs=(P("seq", None), P("seq", "head"), P("seq", "head"), P("seq", "head")),
        check_vma=False,
    )
```

```python
import functools
import math

import jax
import jax.numpy as jnp
from jax import lax
from jax.experimental import pallas as pl
from jax.experimental.pallas import tpu as pltpu
from jax.sharding import PartitionSpec as P

MESH = pl.DeviceIdType.MESH
F32 = jnp.float32
BF16 = jnp.bfloat16
ROWS = 16
VMEM_BYTES = 32 * 1024 * 1024


def iota(shape, dim):
    return lax.broadcasted_iota(jnp.int32, shape, dim)


def nn(a, b):
    return jnp.dot(a, b, preferred_element_type=F32)


def nt(a, b):
    return lax.dot_general(a, b, (((1,), (1,)), ((), ())), preferred_element_type=F32)


def kernel(
    n, pad, scaling,
    og_hbm, expert_hbm, counts_hbm, up_hbm, down_hbm, pre_hbm, q_hbm, k_hbm, v_hbm, wout_hbm,
    gh, gq, gk, gv,
    expert_of, counts, up, down, pre, wout, q, k, v, mask, grad_t, xsend, x, hsum,
    ysend, yrecv, rsend, ret, part, part_in, grads, wall, head_send, head_recv,
    ks_send, ks_recv, ks, qs_send, qs_recv, qs,
    load_sem, one_send, one_recv, disp_send, disp_recv, ax_send, ax_recv,
    hy_send, hy_recv, ret_send, ret_recv, st_send, st_recv, wall_send, wall_recv, head_ssem, head_rsem,
):
    s = lax.axis_index("seq")
    h = lax.axis_index("head")
    c = lax.rem(h, 2)
    y = lax.div(h, 2)
    sib = (s, h + 1 - 2 * c)
    far = (s, lax.rem(h + 2, 4))
    diag = (s, lax.rem(sib[1] + 2, 4))
    m = n // 2
    width, tok = og_hbm.shape
    pair = 2 * width
    rows = m * pad
    depth = x.shape[2]
    piece = ks.shape[1]
    mine = pl.ds(pl.multiple_of(y * pair, 128), pair)
    other = pl.ds(pl.multiple_of((1 - y) * pair, 128), pair)
    parity = lax.rem(s + c, 2)
    own_rows = pl.ds(pl.multiple_of(c * width, ROWS), width)
    sib_rows = pl.ds(pl.multiple_of((1 - c) * width, ROWS), width)

    def send(src, dst, ssem, rsem, to):
        return pltpu.make_async_remote_copy(
            src_ref=src, dst_ref=dst, send_sem=ssem, recv_sem=rsem, device_id=to, device_id_type=MESH
        )

    barrier = pltpu.get_barrier_semaphore()
    peers = [lax.rem(s + d, n) for d in range(1, n)]
    for p in peers:
        pl.semaphore_signal(barrier, inc=1, device_id=(p, h), device_id_type=MESH)
    for to in (sib, far, diag):
        pl.semaphore_signal(barrier, inc=1, device_id=to, device_id_type=MESH)
    loads = {}
    for i, (name, src, dst) in enumerate((
        ("expert", expert_hbm, expert_of), ("grad", og_hbm, grad_t.at[own_rows]),
        ("wout", wout_hbm, wout), ("k", k_hbm, k), ("v", v_hbm, v), ("counts", counts_hbm, counts),
        ("pre", pre_hbm, pre.at[0]), ("down", down_hbm.at[0], down.at[0]),
        ("up", up_hbm.at[0], up.at[0]),
        ("q", q_hbm, q),
    )):
        loads[name] = pltpu.make_async_copy(src, dst, load_sem.at[i])
        loads[name].start()

    pl.semaphore_wait(barrier, n + 2)
    pending = []

    def start(copy):
        copy.start()
        pending.append(copy)
        return copy

    loads["grad"].wait()
    spot = grad_t.at[own_rows]
    start(send(spot, spot, one_send.at[0], one_recv.at[0], sib))
    cut = n * piece // 2

    def wall_rows(k):
        return pl.ds(k * cut, cut)

    def wall_swap(k):
        start(send(
            wout.at[wall_rows(k), other], wall.at[h, wall_rows(k)],
            wall_send.at[k], wall_recv.at[k], far,
        ))

    def wall_relay(k):
        spot = wall.at[far[1], wall_rows(k)]
        send(spot, spot, wall_send.at[k], wall_recv.at[k], far).wait_recv()
        start(send(spot, spot, wall_send.at[3 + k], wall_recv.at[3 + k], sib))

    loads["wout"].wait()
    wall_swap(0)

    loads["expert"].wait()
    e_row = expert_of[...]
    eye = iota((tok, tok), 0) == iota((tok, tok), 1)
    e_col = jnp.sum(jnp.where(eye, e_row, 0), axis=1, keepdims=True)
    same = (e_col == e_row).astype(jnp.int32)
    below = iota((tok, tok), 0) < iota((tok, tok), 1)
    rank_row = jnp.sum(jnp.where(below, same, 0), axis=0, keepdims=True)
    live_row = lax.rem(e_row, 2) == parity
    slot_row = jnp.where(live_row, lax.div(e_row, 2) * pad + rank_row, -1)
    scatter = (iota((rows, tok), 0) == slot_row).astype(BF16)

    swaps = []
    for i, (name, both) in enumerate((("pre", pre), ("down", down), ("up", up))):
        loads[name].wait()
        swaps.append(start(send(both.at[0], both.at[1], one_send.at[3 + i], one_recv.at[3 + i], sib)))

    wall[h] = wout[:, mine]
    start(send(wout.at[:, mine], wall.at[h], wall_send.at[2], wall_recv.at[2], sib))

    spot = grad_t.at[sib_rows]
    send(spot, spot, one_send.at[0], one_recv.at[0], sib).wait_recv()
    blocks = nt(scatter, grad_t[...]).astype(BF16)
    for i in range(m):
        xsend[i] = blocks[i * pad : (i + 1) * pad]
    turns = [*range(1, m), 0]
    order = [(j, lax.rem(s + c + 2 * j, n)) for j in turns]
    for j, p in order:
        copy = send(
            xsend.at[lax.div(p, 2)], x.at[lax.div(s, 2), :, mine],
            disp_send.at[j], disp_recv.at[lax.div(s, 2)], (p, h),
        )
        if j == 0:
            pl.when(c == 1)(copy.start)

            @pl.when(c == 0)
            def _():
                x[lax.div(s, 2), :, mine] = xsend[lax.div(s, 2)]
        else:
            start(copy)

    loads["counts"].wait()
    slot = iota((rows, 1), 0)
    source = 2 * lax.div(slot, pad) + parity
    before = iota((rows, n), 1) < source
    packed = jnp.sum(jnp.where(before, counts[...], 0), axis=1, keepdims=True) + lax.rem(slot, pad)
    unpack = (iota((rows, pre.shape[1]), 1) == packed).astype(BF16)
    mask[0] = nn(unpack, pre[0]).astype(BF16).reshape(m, pad, -1)

    near = [(j, lax.rem(s + c + 2 * j, n)) for j in sorted(range(m), key=lambda j: min(j, m - j))]
    for j, p in near:
        i = lax.div(p, 2)
        spot = x.at[i, :, mine]
        copy = send(spot, spot, disp_send.at[j], disp_recv.at[i], (p, h))
        if j == 0:
            pl.when(c == 1)(copy.wait_recv)
        else:
            copy.wait_recv()
        start(send(spot, spot, ax_send.at[j], ax_recv.at[j], far))

    wall_relay(0)

    loads["k"].wait()
    loads["v"].wait()
    ks_part = nn(k[...].T, v[...]).astype(BF16)
    for p in range(n):
        ks_send[p] = ks_part[p * piece : (p + 1) * piece]

    def state_scatter(at, source, dest):
        for d, p in enumerate(peers):
            start(send(source.at[p], dest.at[s], st_send.at[at, d], st_recv.at[at, s], (p, h)))
        dest[s] = source[s]

    def state_sum(at, dest, total):
        for p in peers:
            send(dest.at[p], dest.at[p], st_send.at[at, 0], st_recv.at[at, p], (p, h)).wait_recv()
        acc = dest[0].astype(F32)
        for p in range(1, n):
            acc = acc + dest[p].astype(F32)
        total[s] = acc.astype(BF16)
        for d, p in enumerate(peers):
            start(send(
                total.at[s], total.at[s], st_send.at[at + 1, d], st_recv.at[at + 1, s], (p, h)
            ))

    def state_wait(at, total):
        for p in peers:
            send(total.at[p], total.at[p], st_send.at[at, 0], st_recv.at[at, p], (p, h)).wait_recv()

    state_scatter(0, ks_send, ks_recv)

    group = max(m // 2, 1)
    groups = [
        [(j, lax.div(p, 2)) for j, p in near[g : g + group]] for g in range(0, m, group)
    ]
    firsts = [jnp.concatenate([x[i, :, mine] for _, i in some], axis=0) for some in groups]
    middles = [[nt(ready, down[0, :, mine])] for ready in firsts]
    swaps[0].wait_recv()
    mask[1] = nn(unpack, pre[1]).astype(BF16).reshape(m, pad, -1)
    swaps[1].wait_recv()
    for middle, ready in zip(middles, firsts):
        middle.append(nt(ready, down[1, :, mine]))
    swaps[2].wait_recv()
    mids = []
    for some, middle in zip(groups, middles):
        for j, i in some:
            spot = x.at[i, :, other]
            send(spot, spot, ax_send.at[j], ax_recv.at[j], far).wait_recv()
        ready = jnp.concatenate([x[i, :, other] for _, i in some], axis=0)
        mid = []
        for u in range(2):
            full_sum = middle[u] + nt(ready, down[u, :, other])
            live = jnp.concatenate([mask[u, i] for _, i in some], axis=0)
            mid.append(jnp.where(live > 0, full_sum, 0.0).astype(BF16))
        away = (nt(mid[0], up[0, other, :]) + nt(mid[1], up[1, other, :])).astype(BF16)
        for at, (j, i) in enumerate(some):
            ysend[i] = away[at * pad : (at + 1) * pad]
            start(send(ysend.at[i], yrecv.at[i], hy_send.at[j], hy_recv.at[j], far))
        mids.append((some, mid))
        if len(mids) == 1:
            state_sum(0, ks_recv, ks)
    wall_swap(1)
    for some, mid in mids:
        stay = nt(mid[0], up[0, mine, :]) + nt(mid[1], up[1, mine, :])
        for at, (j, i) in enumerate(some):
            hsum[i] = stay[at * pad : (at + 1) * pad]

    for j, p in near:
        i = lax.div(p, 2)
        spot = yrecv.at[i]
        send(spot, spot, hy_send.at[j], hy_recv.at[j], far).wait_recv()
        rsend[i] = (hsum[i] + yrecv[i].astype(F32)).astype(BF16)
        copy = send(
            rsend.at[i], ret.at[lax.div(s, 2)], ret_send.at[j], ret_recv.at[lax.div(s, 2)], (p, h)
        )
        if j == 0:
            pl.when(c == 1)(copy.start)

            @pl.when(c == 0)
            def _():
                ret[lax.div(s, 2)] = rsend[lax.div(s, 2)]
        else:
            start(copy)
    above = iota((tok, tok), 1) < iota((tok, tok), 0)
    rank_col = jnp.sum(jnp.where(above, same, 0), axis=1, keepdims=True)
    live_col = lax.rem(e_col, 2) == parity
    slot_col = jnp.where(live_col, lax.div(e_col, 2) * pad + rank_col, -1)
    combine = (iota((tok, rows), 1) == slot_col).astype(BF16)
    own = jnp.where(live_col, grad_t[...].astype(F32).T, 0.0)
    loads["q"].wait()
    q_t = q[...].T
    wall_relay(1)
    spot = wall.at[sib[1]]
    send(spot, spot, wall_send.at[2], wall_recv.at[2], sib).wait_recv()
    for b in range(2):
        spot = wall.at[diag[1], wall_rows(b)]
        send(spot, spot, wall_send.at[3 + b], wall_recv.at[3 + b], sib).wait_recv()
    for j, p in near:
        i = lax.div(p, 2)
        copy = send(ret.at[i], ret.at[i], ret_send.at[j], ret_recv.at[i], (p, h))
        if j == 0:
            pl.when(c == 1)(copy.wait_recv)
        else:
            copy.wait_recv()
    half = (own + nn(combine, ret[...].reshape(rows, pair))).astype(BF16)
    dim = n * piece
    for b in range(2):
        for i, to in enumerate((diag, far, sib)):
            head_send[b, i] = nt(half, wall[to[1], b * cut : (b + 1) * cut, :]).astype(BF16)
            start(send(
                head_send.at[b, i], head_recv.at[b, i], head_ssem.at[b, i], head_rsem.at[b, i], to
            ))
    part[...] = half
    start(send(part, part_in, one_send.at[1], one_recv.at[1], sib))
    head_grad = []
    for b in range(2):
        head_sum = nt(half, wall[h, b * cut : (b + 1) * cut, :])
        for i, to in ((2, sib), (1, far), (0, diag)):
            spot = head_recv.at[b, i]
            send(spot, spot, head_ssem.at[b, i], head_rsem.at[b, i], to).wait_recv()
            head_sum = head_sum + head_recv[b, i].astype(F32)
        head_grad.append(head_sum.astype(BF16))
        qs_part = nn(q_t, head_grad[b]).astype(BF16)
        for p in range(n):
            qs_send[b, p] = qs_part[p * piece : (p + 1) * piece]
        state_scatter(2 + 2 * b, qs_send.at[b], qs_recv.at[b])
    send(part, part_in, one_send.at[1], one_recv.at[1], sib).wait_recv()
    grads[:, mine] = part[...] + part_in[...]
    spot = grads.at[:, mine]
    start(send(spot, spot, one_send.at[2], one_recv.at[2], far))
    state_wait(1, ks)
    k_round = ks[...].reshape(dim, dim)
    gq[...] = (
        scaling * (nt(head_grad[0], k_round[:, :cut]) + nt(head_grad[1], k_round[:, cut:]))
    ).astype(BF16)
    for b in range(2):
        state_sum(2 + 2 * b, qs_recv.at[b], qs.at[b])
    spot = grads.at[:, other]
    send(spot, spot, one_send.at[2], one_recv.at[2], far).wait_recv()
    gh[...] = grads[...]
    key_sum = 0.0
    for b in range(2):
        state_wait(3 + 2 * b, qs.at[b])
        q_round = qs[b].reshape(dim, cut)
        gv[:, b * cut : (b + 1) * cut] = (scaling * nn(k[...], q_round)).astype(BF16)
        key_sum = key_sum + nt(v[:, b * cut : (b + 1) * cut], q_round)
    gk[...] = (scaling * key_sum).astype(BF16)

    for copy in pending:
        copy.wait_send()

    @pl.when(c == 1)
    def _():
        send(xsend.at[0], xsend.at[0], disp_send.at[0], disp_recv.at[0], sib).wait_send()
        send(rsend.at[0], rsend.at[0], ret_send.at[0], ret_recv.at[0], sib).wait_send()


def write_out(*refs):
    count = len(refs) // 2
    sem = refs[-1]
    copies = [pltpu.make_async_copy(refs[i], refs[count + i], sem.at[i]) for i in range(count)]
    for copy in copies:
        copy.start()
    for copy in copies:
        copy.wait()


def fused(out_grad, expert_of, counts, w_up, w_down, pre_act, queries, keys, values, w_out):
    n = lax.axis_size("seq")
    m = n // 2
    tok, width = out_grad.shape
    slots = pre_act.shape[0]
    cap = slots // n
    pad = -(-cap // ROWS) * ROWS
    rows = m * pad
    depth, hidden = w_up.shape[1:]
    dim = queries.shape[1]
    pair = 2 * width
    piece = dim // n
    scaling = 1.0 / math.sqrt(dim * tok * n)
    hbm = pl.BlockSpec(memory_space=pltpu.HBM)
    vmem = pl.BlockSpec(memory_space=pltpu.VMEM)
    dma = pltpu.SemaphoreType.DMA

    def buf(*shape, dtype=BF16):
        return pltpu.VMEM(shape, dtype)

    state = buf(n, piece, dim)
    halves = buf(2, n, piece, dim // 2)
    out = jax.ShapeDtypeStruct((tok, dim), BF16)
    outs = (jax.ShapeDtypeStruct((tok, depth), BF16), out, out, out)
    results = pl.pallas_call(
        functools.partial(kernel, n, pad, scaling),
        out_shape=outs,
        in_specs=[hbm] * 10,
        out_specs=(vmem,) * 4,
        scratch_shapes=[
            buf(1, tok, dtype=jnp.int32), buf(1, n, dtype=jnp.int32),
            buf(2, depth, hidden), buf(2, hidden, depth), buf(2, slots, hidden), buf(dim, depth),
            buf(tok, dim), buf(tok, dim), buf(tok, dim), buf(2, m, pad, hidden),
            buf(pair, tok), buf(m, pad, pair), buf(m, pad, depth), buf(m, pad, pair, dtype=F32),
            buf(m, pad, pair), buf(m, pad, pair), buf(m, pad, pair), buf(m, pad, pair),
            buf(tok, pair), buf(tok, pair), buf(tok, depth),
            buf(4, dim, pair), buf(2, 3, tok, dim // 2), buf(2, 3, tok, dim // 2),
            state, state, state, halves, halves, halves,
            dma((10,)), dma((6,)), dma((6,)), dma((m,)), dma((m,)), dma((m,)), dma((m,)),
            dma((m,)), dma((m,)), dma((m,)), dma((m,)), dma((6, n)), dma((6, n)), dma((5,)), dma((5,)),
            dma((2, 3)), dma((2, 3)),
        ],
        compiler_params=pltpu.CompilerParams(
            collective_id=0, has_side_effects=True, vmem_limit_bytes=VMEM_BYTES
        ),
    )(*(pltpu.with_memory_space_constraint(operand, pltpu.HBM) for operand in (
        out_grad.T, expert_of.reshape(1, tok), counts.T, w_up, w_down, pre_act,
        queries, keys, values, w_out,
    )))
    return pl.pallas_call(
        write_out,
        out_shape=outs,
        in_specs=[vmem] * 4,
        out_specs=(hbm,) * 4,
        scratch_shapes=[dma((4,))],
        compiler_params=pltpu.CompilerParams(vmem_limit_bytes=VMEM_BYTES // 8),
    )(*results)


def step(*arrays):
    n, heads = lax.axis_size("seq"), lax.axis_size("head")
    width, dim = arrays[0].shape[1], arrays[6].shape[1]
    fits = heads == 4 and n % 2 == 0 and dim % (n * ROWS) == 0 and dim % 256 == 0 and 2 * width % 128 == 0
    return (fused if fits else shards)(*arrays)


def shards(out_grad, expert_of, counts, w_up, w_down, pre_act, queries, keys, values, w_out):
    experts = lax.axis_size("seq")
    tok_rows = out_grad.shape[0]
    slot_count = pre_act.shape[0]
    capacity = slot_count // experts
    head_dim = queries.shape[1]
    scaling = 1.0 / math.sqrt(head_dim * tok_rows * experts)
    full_rows = lax.all_gather(out_grad, "head", axis=1, tiled=True)
    expert_ids = jnp.arange(experts, dtype=jnp.int32)
    onehot = (expert_of[:, None] == expert_ids[None, :]).astype(jnp.int32)
    token_rank = jnp.sum((jnp.cumsum(onehot, axis=0) - 1) * onehot, axis=1)
    slot_of = expert_of * capacity + token_rank
    token_of_slot = (
        jnp.full((experts * capacity,), tok_rows, jnp.int32)
        .at[slot_of]
        .set(jnp.arange(tok_rows, dtype=jnp.int32))
    )
    arrived = counts[:, 0]
    offsets = jnp.cumsum(arrived) - arrived
    arrived_total = jnp.sum(arrived)
    packed_ids = jnp.arange(slot_count, dtype=jnp.int32)
    source = jnp.sum((offsets[None, :] <= packed_ids[:, None]).astype(jnp.int32), axis=1) - 1
    within = packed_ids - offsets[source]
    packed_live = packed_ids < arrived_total
    flat_pos = jnp.where(packed_live, source * capacity + within, experts * capacity)
    down_local = w_down[0]
    up_local = w_up[0]
    padded = jnp.concatenate(
        [full_rows, jnp.zeros((1, full_rows.shape[1]), full_rows.dtype)], axis=0
    )
    received = lax.all_to_all(
        padded[token_of_slot].reshape(experts, capacity, full_rows.shape[1]),
        "seq",
        split_axis=0,
        concat_axis=0,
        tiled=True,
    )
    flat_rows = received.reshape(experts * capacity, received.shape[2])
    padded = jnp.concatenate(
        [flat_rows, jnp.zeros((1, flat_rows.shape[1]), flat_rows.dtype)], axis=0
    )
    middle = jnp.dot(padded[flat_pos], down_local.T, preferred_element_type=jnp.float32)
    mid_grad = jnp.where(pre_act > 0, middle, jnp.zeros_like(middle)).astype(jnp.bfloat16)
    hidden_part = jnp.dot(mid_grad, up_local.T, preferred_element_type=jnp.float32)
    slot_ids = jnp.arange(experts * capacity, dtype=jnp.int32)
    slot_source = slot_ids // capacity
    slot_rank = slot_ids % capacity
    slot_live = slot_rank < arrived[slot_source]
    slot_pos = jnp.where(slot_live, offsets[slot_source] + slot_rank, slot_count)
    share_packed = lax.psum_scatter(
        hidden_part.astype(jnp.bfloat16), "head", scatter_dimension=1, tiled=True
    )
    share_width = share_packed.shape[1]
    padded_grad = jnp.concatenate(
        [share_packed, jnp.zeros((1, share_packed.shape[1]), jnp.bfloat16)], axis=0
    )
    returned = lax.all_to_all(
        padded_grad[slot_pos].reshape(experts, capacity, share_packed.shape[1]),
        "seq",
        split_axis=0,
        concat_axis=0,
        tiled=True,
    )
    share_grad = returned.reshape(experts * capacity, share_width)[slot_of]
    expert_grad = lax.all_gather(share_grad, "head", axis=1, tiled=True)
    grad_hidden = (full_rows.astype(jnp.float32) + expert_grad.astype(jnp.float32)).astype(
        jnp.bfloat16
    )
    head_grad = jnp.dot(grad_hidden, w_out.T, preferred_element_type=jnp.float32).astype(
        jnp.bfloat16
    )
    query_part = jnp.dot(queries.T, head_grad, preferred_element_type=jnp.float32)
    key_state, query_state = lax.psum(
        (jnp.dot(keys.T, values, preferred_element_type=jnp.float32), query_part), "seq"
    )
    key_round = key_state.astype(jnp.bfloat16)
    query_round = query_state.astype(jnp.bfloat16)
    grad_queries = (
        scaling * jnp.dot(head_grad, key_round.T, preferred_element_type=jnp.float32)
    ).astype(jnp.bfloat16)
    grad_keys = (
        scaling * jnp.dot(values, query_round.T, preferred_element_type=jnp.float32)
    ).astype(jnp.bfloat16)
    grad_values = (scaling * jnp.dot(keys, query_round, preferred_element_type=jnp.float32)).astype(
        jnp.bfloat16
    )
    return (grad_hidden, grad_queries, grad_keys, grad_values)


def solution(mesh):
    return jax.shard_map(
        step,
        mesh=mesh,
        in_specs=(
            P("seq", "head"),
            P("seq"),
            P(None, "seq"),
            P("seq", None, "head"),
            P("seq", "head", None),
            P("seq", "head"),
            P("seq", "head"),
            P("seq", "head"),
            P("seq", "head"),
            P("head", None),
        ),
        out_specs=(P("seq", None), P("seq", "head"), P("seq", "head"), P("seq", "head")),
        check_vma=False,
    )
```
